32 devices in a mesh: rep: 2 (over x), shard: 16 (over z, y, core).
Axes of the slice: x: 2, y: 2, z: 4, core: 2. Of those that a mesh axis runs over, the one named last changes fastest.
Arguments:
- tokens: bfloat16 [8192, 2048], P(('rep', 'shard')), may hold values from -6 to 6
- doc_ids: int32 [8192], P(('rep', 'shard')), may hold values from 0 to 31, as said below
- cotangent: bfloat16 [8192, 2048], P(('rep', 'shard')), may hold values from -6 to 6
- ln1_gain: bfloat16 [2048], P('shard'), may hold values from 0.5 to 1.5
- ln1_bias: bfloat16 [2048], P('shard'), may hold values from -1.25 to 1.25
- w_qkv: bfloat16 [2048, 6144], P('shard'), may hold values from -0.125 to 0.125
- b_qkv: bfloat16 [6144], P('shard'), may hold values from -1.75 to 1.75
- w_out: bfloat16 [2048, 2048], P('shard'), may hold values from -0.5 to 0.5
- ln2_gain: bfloat16 [2048], P('shard'), may hold values from 0.5 to 1.5
- ln2_bias: bfloat16 [2048], P('shard'), may hold values from -1.25 to 1.25
- w_gate: bfloat16 [2048, 5632], P('shard'), may hold values from -0.125 to 0.125
- w_up: bfloat16 [2048, 5632], P('shard'), may hold values from -0.125 to 0.125
- w_down: bfloat16 [5632, 2048], P('shard'), may hold values from -0.078125 to 0.078125
Outputs:
- activations: bfloat16 [8192, 2048], P(('rep', 'shard'))
- d_tokens: float32 [8192, 2048], P(('rep', 'shard'))
- grad_ln1_gain: float32 [2048], P('shard')
- grad_ln1_bias: float32 [2048], P('shard')
- grad_w_qkv: float32 [2048, 6144], P('shard')
- grad_b_qkv: float32 [6144], P('shard')
- grad_w_out: float32 [2048, 2048], P('shard')
- grad_ln2_gain: float32 [2048], P('shard')
- grad_ln2_bias: float32 [2048], P('shard')
- grad_w_gate: float32 [2048, 5632], P('shard')
- grad_w_up: float32 [2048, 5632], P('shard')
- grad_w_down: float32 [5632, 2048], P('shard')
The draws below stay inside these ranges and needn't reach their ends.
Inputs may be any that keep to these rules, and one draw needn't show every extreme that they name: `doc_ids`: within each device's 256 tokens the numbers start at 0 and rise by one at each new document; documents never cross devices; in every draw some device holds a single document of 256 tokens, and some device holds the largest number of documents.
All inputs are finite; a program needn't handle non-finite values.
Results may differ from the reference program's by a relative error of at most 0.014.
Values may be sent and summed in bfloat16 or wider, within the bound.
No kernel may reach another device: no remote copies, remote signals or barrier semaphores. Data moves between devices by JAX's collectives and lax.ppermute only.
A program may use at most 640 MiB of HBM per device.

```python
import jax
import jax.numpy as jnp
from jax import lax

D = 2048
FF = 5632
HEADS = 32
HEAD_DIM = 64
ROT = 16
TOK_DEV = 256
TOKENS = 8192


def draw_doc_ids(key, part):
    key = jax.random.fold_in(key, 7)
    blocks = TOKENS // TOK_DEV
    most_docs = min(32, TOK_DEV // 4)
    exp_key, count_key, perm_key, pick_key = jax.random.split(key, 4)
    exponent = jax.random.randint(exp_key, (blocks,), 0, 6)
    limits = jnp.left_shift(jnp.ones((blocks,), jnp.int32), exponent)
    doc_counts = 1 + jax.random.randint(count_key, (blocks,), 0, limits)
    doc_counts = jnp.minimum(doc_counts, most_docs)
    busiest = jax.random.randint(pick_key, (), 1, blocks)
    doc_counts = doc_counts.at[busiest].set(most_docs)
    doc_counts = doc_counts.at[0].set(1)
    perm_keys = jax.random.split(perm_key, blocks)
    orders = jax.vmap(lambda subkey: jax.random.permutation(subkey, TOK_DEV - 1))(perm_keys)
    ranks = jnp.argsort(orders, axis=1)
    start_marks = (ranks < doc_counts[:, None] - 1).astype(jnp.int32)
    start_marks = jnp.concatenate([jnp.zeros((blocks, 1), jnp.int32), start_marks], 1)
    numbers = jnp.cumsum(start_marks, 1).astype(jnp.int32)
    return numbers.reshape(-1)


def block_scale(rng, shape, cuts, low, largest):
    def one(position, blocks):
        steps = jax.random.uniform(jax.random.fold_in(jax.random.fold_in(rng, 6), position), (blocks,), jnp.float32, low / len(cuts), largest / len(cuts))
        return jnp.repeat(jnp.exp(steps), shape[position] // blocks).reshape((-1,) + (1,) * (len(shape) - position - 1))

    loudness = one(*cuts[0])
    for cut in cuts[1:]:
        loudness = loudness * one(*cut)
    return loudness


def normal_values(stream_key, shape, deviation, bound, cuts=(), held_as=jnp.bfloat16):
    array = deviation * jax.random.normal(stream_key, shape, jnp.float32)
    if cuts:
        array = array * block_scale(stream_key, shape, cuts, -0.22, 0.18)
    return jnp.clip(array, -bound, bound).astype(held_as)


def setup_inputs(seed: int = 0) -> dict:
    keys = jax.random.split(jax.random.key(seed), 14)
    tokens = normal_values(keys[0], (TOKENS, D), 1.0, 6.0, ((0, 32),))
    doc_ids = draw_doc_ids(jax.random.fold_in(keys[13], 71), 0)
    cotangent = normal_values(keys[2], (TOKENS, D), 1.0, 6.0, ((0, 32),))
    ln1_gain = jnp.clip(1.0 + 0.1 * jax.random.normal(keys[3], (D,), jnp.float32), 0.5, 1.5).astype(jnp.bfloat16)
    ln1_bias = normal_values(keys[4], (D,), 0.2, 1.25, ((0, 16),))
    w_qkv = normal_values(keys[5], (D, 3 * D), D ** -0.5, 0.125, ((0, 16),))
    b_qkv = normal_values(keys[6], (3 * D,), 0.3, 1.75, ((0, 16),))
    w_out = normal_values(keys[7], (D, D), (D // 16) ** -0.5, 0.5, ((0, 16),))
    ln2_gain = jnp.clip(1.0 + 0.1 * jax.random.normal(keys[8], (D,), jnp.float32), 0.5, 1.5).astype(jnp.bfloat16)
    ln2_bias = normal_values(keys[9], (D,), 0.2, 1.25, ((0, 16),))
    w_gate = normal_values(keys[10], (D, FF), D ** -0.5, 0.125, ((0, 16),))
    w_up = normal_values(keys[11], (D, FF), D ** -0.5, 0.125, ((0, 16),))
    w_down = normal_values(keys[12], (FF, D), FF ** -0.5, 0.078125, ((0, 16),))
    return {"tokens": tokens, "doc_ids": doc_ids, "cotangent": cotangent, "ln1_gain": ln1_gain, "ln1_bias": ln1_bias, "w_qkv": w_qkv, "b_qkv": b_qkv, "w_out": w_out, "ln2_gain": ln2_gain, "ln2_bias": ln2_bias, "w_gate": w_gate, "w_up": w_up, "w_down": w_down}


HIGH = lax.Precision.HIGHEST

@jax.custom_vjp
def low(v):
    return lax.optimization_barrier(v.astype(jnp.bfloat16)).astype(jnp.float32)

@jax.custom_vjp
def low_back(v):
    return v

def low_keep(v):
    return (low(v), None)

def low_pass(kept, grad):
    return (grad,)

def back_keep(v):
    return (v, None)

def back_low(kept, grad):
    return (low(grad),)
low.defvjp(low_keep, low_pass)
low_back.defvjp(back_keep, back_low)

def matmul(left, right):
    return jnp.dot(left, right, precision=HIGH, preferred_element_type=jnp.float32)

def layer_norm(values, gain_vec, bias_vec):
    average = lax.optimization_barrier(jnp.mean(values, -1, keepdims=True))
    centered = values - average
    spread = lax.optimization_barrier(jnp.mean(centered * centered, -1, keepdims=True))
    return centered * lax.rsqrt(spread + 1e-05) * gain_vec + bias_vec

def rotate(values, cos_table, sin_table):
    half_rot = ROT // 2
    cos_heads = cos_table[..., None, :]
    sin_heads = sin_table[..., None, :]
    first_part = values[..., :half_rot]
    second = values[..., half_rot:ROT]
    return jnp.concatenate([first_part * cos_heads - second * sin_heads, second * cos_heads + first_part * sin_heads, values[..., ROT:]], -1)

def block_positions(doc_block):
    length = doc_block.shape[0]
    indices = jnp.arange(length, dtype=jnp.int32)
    same_doc = doc_block[:, None] == doc_block[None, :]
    first_row = lax.optimization_barrier(jnp.min(jnp.where(same_doc, indices[None, :], length), axis=1)).astype(jnp.int32)
    allowed = same_doc & (indices[None, :] <= indices[:, None])
    return (indices - first_row, allowed)

def attend_block(inputs):
    query_blk, key_blk, value_blk, allowed = inputs
    raw_scores = jnp.einsum('thd,shd->hts', query_blk, key_blk, precision=HIGH)
    scores = low_back(raw_scores) * 0.125
    scores = jnp.where(allowed[None], scores, -1e+30)
    highest = lax.optimization_barrier(jnp.max(scores, -1, keepdims=True))
    exp_scores = jnp.exp(scores - highest)
    attn_probs = low(exp_scores / lax.optimization_barrier(jnp.sum(exp_scores, -1, keepdims=True)))
    return jnp.einsum('hts,shd->thd', attn_probs, value_blk, precision=HIGH)

def reference(tokens, doc_ids, cotangent, ln1_gain, ln1_bias, w_qkv, b_qkv, w_out, ln2_gain, ln2_bias, w_gate, w_up, w_down):
    blocks = doc_ids.shape[0] // TOK_DEV
    positions, allowed = jax.vmap(block_positions)(doc_ids.reshape(blocks, TOK_DEV))
    frequency = 10000.0 ** (-(jnp.arange(ROT // 2, dtype=jnp.float32) * 2.0 / ROT))
    angles = positions.astype(jnp.float32)[..., None] * frequency
    cos_table = jnp.cos(angles)
    sin_table = jnp.sin(angles)

    def forward(inputs, gain_one, bias_one, weight_qkv, bias_qkv, weight_out, gain_two, bias_two, weight_gate, weight_up, weight_down):
        normed = low(layer_norm(inputs, gain_one, bias_one))
        projected = low_back(matmul(normed, weight_qkv) + bias_qkv)
        head_split = projected.reshape(blocks, TOK_DEV, 3, HEADS, HEAD_DIM)
        query_all = low(rotate(head_split[:, :, 0], cos_table, sin_table))
        key_all = low(rotate(head_split[:, :, 1], cos_table, sin_table))
        value_all = low(head_split[:, :, 2])
        attended = lax.map(jax.checkpoint(attend_block), (query_all, key_all, value_all, allowed))
        attended = low_back(low(attended.reshape(-1, D)))
        hidden = inputs + low_back(matmul(attended, weight_out))
        normed_two = low(layer_norm(hidden, gain_two, bias_two))
        gate_val = low_back(matmul(normed_two, weight_gate))
        up_val = low_back(matmul(normed_two, weight_up))
        mixed = low(jax.nn.silu(gate_val) * up_val)
        return hidden + matmul(mixed, weight_down)
    floats = [arr.astype(jnp.float32) for arr in (tokens, ln1_gain, ln1_bias, w_qkv, b_qkv, w_out, ln2_gain, ln2_bias, w_gate, w_up, w_down)]
    result, backward = jax.vjp(forward, *floats)
    grads = backward(cotangent.astype(jnp.float32))
    return (result.astype(jnp.bfloat16), grads[0], grads[1], grads[2], grads[3], grads[4], grads[5], grads[6], grads[7], grads[8], grads[9], grads[10])
```

```python
import jax
import jax.numpy as jnp
from jax import lax
from jax.sharding import Mesh, PartitionSpec as P

HEAD_DIM = 64
ROT = 16
PLANE = ("x", "y", "c")
EVERY = ("x", "z", "y", "c")
SIBLING = (1, 1)
FIRST = (4, 2)
SECOND = (2, 4)
ACROSS_X = (4, 4)
ACROSS_Y = (2, 2)
ACROSS_YC = (3, 3)


def swap(values, masks):
    pairs = [(i, i ^ masks[i & 1]) for i in range(8)]
    return lax.ppermute(values, PLANE, pairs)


def plane_gather(values):
    near = swap(values, FIRST)
    side = swap(values, SECOND)
    far = swap(near, SECOND)
    own = [values, near, side, far]
    return own + [swap(part, SIBLING) for part in own]


def plane_sum(own, other):
    merged = [
        mine.astype(jnp.float32) + swap(theirs, SIBLING).astype(jnp.float32)
        for mine, theirs in zip(own, other)
    ]
    far = swap(merged[3].astype(jnp.bfloat16), SECOND)
    side = swap(merged[2].astype(jnp.bfloat16), SECOND)
    near = swap((merged[1] + far.astype(jnp.float32)).astype(jnp.bfloat16), FIRST)
    return merged[0] + side.astype(jnp.float32) + near.astype(jnp.float32)


def by_owner(parts, y_index, c_index):
    first, second, third, fourth = parts
    odd = c_index == 1
    first, second = jnp.where(odd, second, first), jnp.where(odd, first, second)
    third, fourth = jnp.where(odd, fourth, third), jnp.where(odd, third, fourth)
    upper = y_index == 1
    return [
        jnp.where(upper, third, first),
        jnp.where(upper, fourth, second),
        jnp.where(upper, first, third),
        jnp.where(upper, second, fourth),
    ]


def exchange(blocks, y_index, c_index):
    mine = by_owner(blocks, y_index, c_index)
    moved = [
        mine[0],
        swap(mine[1], SIBLING),
        swap(mine[2], ACROSS_Y),
        swap(mine[3], ACROSS_YC),
    ]
    return by_owner(moved, y_index, c_index)


def layer_norm(values, gain_vec, bias_vec):
    average = jnp.mean(values, -1, keepdims=True)
    centered = values - average
    recip_std = lax.rsqrt(jnp.mean(centered * centered, -1, keepdims=True) + 1e-05)
    unit_vals = centered * recip_std
    return (unit_vals * gain_vec + bias_vec, unit_vals, recip_std)


def norm_back(grad_in, unit_vals, recip_std, gain_vec):
    scaled = grad_in * gain_vec
    return recip_std * (
        scaled
        - jnp.mean(scaled, -1, keepdims=True)
        - unit_vals * jnp.mean(scaled * unit_vals, -1, keepdims=True)
    )


def rotate(values, cos_table, sin_table):
    half_rot = ROT // 2
    cos_heads = cos_table[:, :, None, :]
    sin_heads = sin_table[:, :, None, :]
    first_part = values[..., :half_rot]
    second = values[..., half_rot:ROT]
    return jnp.concatenate(
        [
            first_part * cos_heads - second * sin_heads,
            second * cos_heads + first_part * sin_heads,
            values[..., ROT:],
        ],
        -1,
    )


def dot(left, right):
    return jnp.dot(left, right, preferred_element_type=jnp.float32)


def contract_last(left, right):
    return lax.dot_general(
        left, right, (((1,), (1,)), ((), ())), preferred_element_type=jnp.float32
    )


def contract_first(left, right):
    return lax.dot_general(
        left, right, (((0,), (0,)), ((), ())), preferred_element_type=jnp.float32
    )


def einsum(spec, left, right):
    return jnp.einsum(spec, left, right, preferred_element_type=jnp.float32)


def gather_z(values):
    return lax.all_gather(values, "z", axis=0, tiled=True)


def scatter_z(values):
    return lax.psum_scatter(values, "z", scatter_dimension=0, tiled=True)


def per_device(
    tokens,
    doc_ids,
    cotangent,
    ln1_gain,
    ln1_bias,
    w_qkv,
    b_qkv,
    w_out,
    ln2_gain,
    ln2_bias,
    w_gate,
    w_up,
    w_down,
):
    x_index, z_index = lax.axis_index("x"), lax.axis_index("z")
    y_index, c_index = lax.axis_index("y"), lax.axis_index("c")
    yc_index = 2 * y_index + c_index
    planes = lax.axis_size("z")
    shards = 4 * planes
    rows = w_qkv.shape[0]
    width = rows * shards
    hidden_dim = w_gate.shape[1]
    piece = hidden_dim // (2 * shards)
    mlp = piece * planes
    head_cols = width // 8
    spread = rows % (2 * HEAD_DIM) == 0
    groups = planes if spread else 1
    unit = head_cols // groups
    length = tokens.shape[0]

    def pick_x(values, axis):
        return lax.dynamic_index_in_dim(values, x_index, axis, keepdims=False)

    def pick_yc(values, axis):
        return lax.dynamic_index_in_dim(values, yc_index, axis, keepdims=False)

    def columns(weight, outer, size):
        view = pick_x(weight.reshape(rows, outer, 4, 2, size), 3)
        blocks = [view[:, :, t].reshape(rows, outer * size) for t in range(4)]
        return jnp.concatenate(exchange(blocks, y_index, c_index), 0)

    full_qkv = gather_z(columns(w_qkv, 3 * groups, unit))
    if spread:
        full_out = gather_z(pick_x(w_out.reshape(2, rows // 2, width), 0))
    else:
        full_out = lax.all_gather(w_out, ("z", "y", "c"), axis=0, tiled=True)
        full_out = pick_x(pick_yc(full_out.reshape(4, 2, unit, width), 0), 0)
    full_gate = gather_z(columns(w_gate, planes, piece))
    full_up = gather_z(columns(w_up, planes, piece))
    full_down = gather_z(pick_x(w_down.reshape(2, piece, width), 0))

    vectors = lax.all_gather(
        jnp.concatenate([ln1_gain, ln1_bias, ln2_gain, ln2_bias, b_qkv]),
        ("z", "y", "c"),
        axis=0,
    ).astype(jnp.float32)
    gain_one, bias_one, gain_two, bias_two = (
        vectors[:, i * rows : (i + 1) * rows].reshape(width) for i in range(4)
    )
    bias_qkv = vectors[:, 4 * rows :].reshape(3 * groups, 4, 2, unit)
    bias_qkv = pick_x(pick_yc(bias_qkv, 1), 1).reshape(3 * head_cols)

    docs = jnp.stack(plane_gather(doc_ids))
    all_tokens = jnp.concatenate(plane_gather(tokens), 0)
    all_cot = jnp.concatenate(plane_gather(cotangent), 0)

    indices = jnp.arange(length, dtype=jnp.int32)
    same_doc = docs[:, :, None] == docs[:, None, :]
    first_row = jnp.min(jnp.where(same_doc, indices[None, None, :], length), axis=2)
    allowed = same_doc & (indices[None, None, :] <= indices[None, :, None])
    frequency = 10000.0 ** (-(jnp.arange(ROT // 2, dtype=jnp.float32) * 2.0 / ROT))
    angles = (indices[None] - first_row).astype(jnp.float32)[:, :, None] * frequency
    cos_table = jnp.cos(angles)
    sin_table = jnp.sin(angles)

    def score_block(query_low, key_low):
        scores = einsum("bthd,bshd->bhts", query_low, key_low) * 0.125
        return jnp.where(allowed[:, None], scores, -1e30)

    def halves(values):
        blocks = values.astype(jnp.bfloat16).reshape(8, length, width)
        return [blocks[i] for i in range(4)], [blocks[i] for i in range(4, 8)]

    normed_one, unit_one, _ = layer_norm(all_tokens.astype(jnp.float32), gain_one, bias_one)
    normed_low = normed_one.astype(jnp.bfloat16)
    projected = dot(normed_low, full_qkv) + bias_qkv
    head_split = projected.reshape(8, length, 3, head_cols // HEAD_DIM, HEAD_DIM)
    query_low = rotate(head_split[:, :, 0], cos_table, sin_table).astype(jnp.bfloat16)
    key_low = rotate(head_split[:, :, 1], cos_table, sin_table).astype(jnp.bfloat16)
    value_low = head_split[:, :, 2].astype(jnp.bfloat16)
    scores = score_block(query_low, key_low)
    highest = jnp.max(scores, -1, keepdims=True)
    exp_scores = jnp.exp(scores - highest)
    denominator = jnp.sum(exp_scores, -1, keepdims=True)
    attn_probs = exp_scores / denominator
    attended_low = (
        einsum("bhts,bshd->bthd", attn_probs.astype(jnp.bfloat16), value_low)
        .reshape(8 * length, head_cols)
        .astype(jnp.bfloat16)
    )
    inputs = tokens.astype(jnp.float32)
    hidden = inputs + plane_sum(*halves(dot(attended_low, full_out)))
    normed_two, unit_two, scale_two = layer_norm(hidden, gain_two, bias_two)
    two_low = jnp.concatenate(plane_gather(normed_two.astype(jnp.bfloat16)), 0)
    gate_val = dot(two_low, full_gate)
    up_val = dot(two_low, full_up)
    sigmoid_gate = jax.nn.sigmoid(gate_val)
    silu_gate = gate_val * sigmoid_gate
    mixed_low = (silu_gate * up_val).astype(jnp.bfloat16)
    down_sum = scatter_z(contract_first(mixed_low, all_cot).astype(jnp.bfloat16))
    grad_mixed = contract_last(all_cot, full_down)
    dgate_low = (
        grad_mixed * up_val * sigmoid_gate * (1.0 + gate_val * (1.0 - sigmoid_gate))
    ).astype(jnp.bfloat16)
    dup_low = (grad_mixed * silu_gate).astype(jnp.bfloat16)
    gate_sum = scatter_z(contract_first(two_low, dgate_low).astype(jnp.bfloat16))
    up_sum = scatter_z(contract_first(two_low, dup_low).astype(jnp.bfloat16))
    grad_norm_two = plane_sum(
        *halves(contract_last(dgate_low, full_gate) + contract_last(dup_low, full_up))
    )
    activations = (hidden + plane_sum(*halves(dot(mixed_low, full_down)))).astype(jnp.bfloat16)
    grad_gain_two = jnp.sum(grad_norm_two * unit_two, 0)
    grad_bias_two = jnp.sum(grad_norm_two, 0)
    grad_hidden = cotangent.astype(jnp.float32) + norm_back(
        grad_norm_two, unit_two, scale_two, gain_two
    )
    hidden_low = jnp.concatenate(plane_gather(grad_hidden.astype(jnp.bfloat16)), 0)
    out_part = contract_first(attended_low, hidden_low).astype(jnp.bfloat16)
    datt_low = (
        contract_last(hidden_low, full_out)
        .reshape(8, length, head_cols // HEAD_DIM, HEAD_DIM)
        .astype(jnp.bfloat16)
    )
    grad_value = einsum("bhts,bthd->bshd", attn_probs.astype(jnp.bfloat16), datt_low)
    grad_probs = einsum("bthd,bshd->bhts", datt_low, value_low)
    inner_sum = jnp.sum(attn_probs * grad_probs, -1, keepdims=True)
    grad_scores_low = (0.125 * attn_probs * (grad_probs - inner_sum)).astype(jnp.bfloat16)
    grad_query = einsum("bhts,bshd->bthd", grad_scores_low, key_low)
    grad_key = einsum("bhts,bthd->bshd", grad_scores_low, query_low)
    grad_query = rotate(grad_query, cos_table, -sin_table)
    grad_key = rotate(grad_key, cos_table, -sin_table)
    grad_proj_low = jnp.concatenate(
        [g.reshape(8 * length, head_cols) for g in (grad_query, grad_key, grad_value)], 1
    ).astype(jnp.bfloat16)
    qkv_sum = scatter_z(contract_first(normed_low, grad_proj_low).astype(jnp.bfloat16))
    grad_bqkv = jnp.sum(grad_proj_low, 0, dtype=jnp.float32)
    placed = lax.dynamic_update_slice(
        jnp.zeros((3 * groups, 4, 2, unit), jnp.float32),
        grad_bqkv.reshape(3 * groups, 1, 1, unit),
        (0, yc_index, x_index, 0),
    )
    own, other = halves(contract_last(grad_proj_low, full_qkv))
    grad_norm_one = plane_sum(own, other)
    _, unit_one, scale_one = layer_norm(inputs, gain_one, bias_one)
    grad_gain_one = jnp.sum(grad_norm_one * unit_one, 0)
    grad_bias_one = jnp.sum(grad_norm_one, 0)
    d_tokens = grad_hidden + norm_back(grad_norm_one, unit_one, scale_one, gain_one)

    sums = lax.psum(
        jnp.concatenate(
            [
                grad_gain_one,
                grad_bias_one,
                grad_gain_two,
                grad_bias_two,
                placed.reshape(3 * width),
            ]
        ),
        EVERY,
    )
    shard_index = 4 * z_index + yc_index
    small = [
        lax.dynamic_slice_in_dim(sums[i * width : (i + 1) * width], shard_index * rows, rows)
        for i in range(4)
    ]
    owned_bqkv = lax.dynamic_slice_in_dim(sums[4 * width :], shard_index * 3 * rows, 3 * rows)

    def whole_rows(half):
        other = swap(half, ACROSS_X)
        odd = x_index == 1
        return jnp.concatenate(
            [jnp.where(odd, other, half), jnp.where(odd, half, other)], 0
        ).astype(jnp.float32)

    if spread:
        owned_out = whole_rows(scatter_z(out_part))
    else:
        placed_out = lax.dynamic_update_slice(
            jnp.zeros((4, 2, unit, width), jnp.bfloat16),
            out_part[None, None],
            (yc_index, x_index, 0, 0),
        )
        owned_out = lax.psum_scatter(
            placed_out.reshape(width, width), ("z", "y", "c"), scatter_dimension=0, tiled=True
        )
        owned_out = lax.psum(owned_out, "x").astype(jnp.float32)

    def whole_columns(summed, outer, size):
        blocks = summed.reshape(4, rows, outer * size)
        half = jnp.stack(exchange([blocks[t] for t in range(4)], y_index, c_index))
        other = swap(half, ACROSS_X)
        odd = x_index == 1
        both = jnp.stack([jnp.where(odd, other, half), jnp.where(odd, half, other)])
        both = both.reshape(2, 4, rows, outer, size)
        return both.transpose(2, 3, 1, 0, 4).reshape(rows, -1).astype(jnp.float32)

    return (
        activations,
        d_tokens,
        small[0],
        small[1],
        whole_columns(qkv_sum, 3 * groups, unit),
        owned_bqkv,
        owned_out,
        small[2],
        small[3],
        whole_columns(gate_sum, planes, piece),
        whole_columns(up_sum, planes, piece),
        whole_rows(down_sum),
    )


def solution(mesh):
    reps, shards = mesh.shape["rep"], mesh.shape["shard"]
    grid = Mesh(mesh.devices.reshape(reps, shards // 4, 2, 2), EVERY)
    tokens, rows, vector = P(EVERY, None), P(("z", "y", "c"), None), P(("z", "y", "c"))
    return jax.shard_map(
        per_device,
        mesh=grid,
        in_specs=(
            tokens,
            P(EVERY),
            tokens,
            vector,
            vector,
            rows,
            vector,
            rows,
            vector,
            vector,
            rows,
            rows,
            rows,
        ),
        out_specs=(
            tokens,
            tokens,
            vector,
            vector,
            rows,
            vector,
            rows,
            vector,
            vector,
            rows,
            rows,
            rows,
        ),
        check_vma=False,
    )
```

```python
import jax
import jax.numpy as jnp
from jax import lax
from jax.experimental import pallas as pl
from jax.experimental.pallas import tpu as pltpu
from jax.sharding import Mesh, PartitionSpec as P

HEAD_DIM = 64
ROT = 16
PLANE = ("x", "y", "c")
EVERY = ("x", "z", "y", "c")
SIBLING = (1, 1)
FIRST = (4, 2)
SECOND = (2, 4)
ACROSS_X = (4, 4)
ACROSS_Y = (2, 2)
ACROSS_YC = (3, 3)
VMEM_BYTES = 48 << 20
COST = pl.CostEstimate(flops=1 << 20, bytes_accessed=1 << 20, transcendentals=0)


def swap(values, masks):
    pairs = [(i, i ^ masks[i & 1]) for i in range(8)]
    return lax.ppermute(values, PLANE, pairs)


def plane_gather(values):
    near = swap(values, FIRST)
    side = swap(values, SECOND)
    return [values, near, side, swap(near, SECOND)]


def plane_sum(own, near, side, far):
    far = swap(far, SECOND)
    side = swap(side, SECOND)
    near = (near + far.astype(jnp.float32)).astype(jnp.bfloat16)

    def finish():
        return own + side.astype(jnp.float32) + swap(near, FIRST).astype(jnp.float32)

    return near, finish


def with_sibling(values):
    return [values, swap(values, SIBLING)]


def by_owner(parts, y_index, c_index):
    first, second, third, fourth = parts
    odd = c_index == 1
    first, second = jnp.where(odd, second, first), jnp.where(odd, first, second)
    third, fourth = jnp.where(odd, fourth, third), jnp.where(odd, third, fourth)
    upper = y_index == 1
    return [
        jnp.where(upper, third, first),
        jnp.where(upper, fourth, second),
        jnp.where(upper, first, third),
        jnp.where(upper, second, fourth),
    ]


def exchange(blocks, y_index, c_index):
    mine = by_owner(blocks, y_index, c_index)
    moved = [
        mine[0],
        swap(mine[1], SIBLING),
        swap(mine[2], ACROSS_Y),
        swap(mine[3], ACROSS_YC),
    ]
    return by_owner(moved, y_index, c_index)


def rounds(planes):
    bits = planes.bit_length() - 1
    return [("c", 1, 2), ("y", 1, 2)] + [("z", 1 << b, planes) for b in range(bits)]


def meet(values, axis, bit, size):
    return lax.ppermute(values, axis, [(i, i ^ bit) for i in range(size)])


def gather_small(vector, planes):
    held = vector[None]
    for axis, bit, size in rounds(planes):
        other = meet(held, axis, bit, size)
        upper = (lax.axis_index(axis) & bit) != 0
        held = jnp.concatenate(
            [jnp.where(upper, other, held), jnp.where(upper, held, other)], 0
        )
    return held


def gather_rows(block, planes):
    length, place = block.shape[0], lax.axis_index("z")
    whole = jnp.zeros((planes * length, block.shape[1]), block.dtype)
    for k in range(planes):
        part = meet(block, "z", k, planes) if k else block
        whole = lax.dynamic_update_slice(whole, part, ((place ^ k) * length, 0))
    return whole


def sum_small(vector, planes):
    for axis, bit, size in [("x", 1, 2)] + rounds(planes):
        vector = vector + meet(vector, axis, bit, size)
    return vector


def layer_norm(values, gain_vec, bias_vec):
    average = jnp.mean(values, -1, keepdims=True)
    centered = values - average
    recip_std = lax.rsqrt(jnp.mean(centered * centered, -1, keepdims=True) + 1e-05)
    unit_vals = centered * recip_std
    return (unit_vals * gain_vec + bias_vec, unit_vals, recip_std)


def norm_back(grad_in, unit_vals, recip_std, gain_vec):
    scaled = grad_in * gain_vec
    return recip_std * (
        scaled
        - jnp.mean(scaled, -1, keepdims=True)
        - unit_vals * jnp.mean(scaled * unit_vals, -1, keepdims=True)
    )


def dot(left, right):
    return jnp.dot(left, right, preferred_element_type=jnp.float32)


def contract_last(left, right):
    return lax.dot_general(
        left, right, (((1,), (1,)), ((), ())), preferred_element_type=jnp.float32
    )


def contract_first(left, right):
    return lax.dot_general(
        left, right, (((0,), (0,)), ((), ())), preferred_element_type=jnp.float32
    )


def spread_rotary(positions):
    half_rot = ROT // 2
    frequency = 10000.0 ** (-(jnp.arange(half_rot, dtype=jnp.float32) * 2.0 / ROT))
    lane = jnp.arange(2 * HEAD_DIM) % HEAD_DIM
    frequency = jnp.where(lane < ROT, jnp.tile(frequency, 2 * HEAD_DIM // half_rot), 0.0)
    angles = positions.astype(jnp.float32)[:, None] * frequency
    sine = jnp.sin(angles)
    from_right = jnp.where(lane < half_rot, -sine, 0.0)
    from_left = jnp.where(lane < half_rot, 0.0, sine)
    return jnp.cos(angles), from_right, from_left


def turn(values, straight, from_right, from_left):
    cols = values.shape[1]
    times = cols // straight.shape[1]
    wide = [jnp.concatenate([t] * times, 1) for t in (straight, from_right, from_left)]
    half_rot = ROT // 2
    return (
        values * wide[0]
        + pltpu.roll(values, cols - half_rot, 1) * wide[1]
        + pltpu.roll(values, half_rot, 1) * wide[2]
    )


def head_mask(head, shape):
    lane = lax.broadcasted_iota(jnp.int32, shape, 1)
    return (lane >= head * HEAD_DIM) & (lane < (head + 1) * HEAD_DIM)


def visible(docs_col, docs_row):
    shape = (docs_col.shape[0], docs_row.shape[1])
    row = lax.broadcasted_iota(jnp.int32, shape, 0)
    col = lax.broadcasted_iota(jnp.int32, shape, 1)
    return (docs_col == docs_row) & (col <= row)


def head_scores(query, key, mask, allowed):
    picked = jnp.where(mask, query, jnp.zeros_like(query)) * 0.125
    return jnp.where(allowed, contract_last(picked.astype(query.dtype), key), -1e30)


def pick_slot(step, slots, place):
    for k, slot in enumerate(slots):

        @pl.when(step == k)
        def _(slot=slot):
            place[...] = slot[...]


def put_slot(step, value, slots):
    for k, slot in enumerate(slots):

        @pl.when(step == k)
        def _(slot=slot):
            slot[...] = value.astype(slot.dtype)


def loader(step, sources, places, sems):
    def copies(which):
        return [
            pltpu.make_async_copy(sources[which][k], places[k].at[which], sems.at[which, k])
            for k in range(len(places))
        ]

    @pl.when(step == 0)
    def _():
        for which in range(2):
            for copy in copies(which):
                copy.start()

    def wait(which):
        @pl.when(step == 0)
        def _():
            for copy in copies(which):
                copy.wait()

    return wait


def forward_kernel(first, *refs):
    slots, refs = refs[:2], refs[2:]
    gain, bias, proj_bias, docs_col, docs_row, straight, right, left = refs[:8]
    weights = [refs[8:10], refs[10:12]]
    outs, (place, weight, weight_out, sems) = refs[-10:-4], refs[-4:]
    normed, proj, lse, attended = outs[:4]
    step = pl.program_id(0)
    wait = loader(step, weights, [weight, weight_out], sems)
    pick_slot(step, slots, place)
    values, _, _ = layer_norm(place[...].astype(jnp.float32), gain[...], bias[...])
    low = values.astype(jnp.bfloat16)
    normed[...] = low
    allowed = visible(docs_col[0], docs_row[0])
    lane = lax.broadcasted_iota(jnp.int32, lse.shape, 1)
    logs = jnp.zeros(lse.shape, jnp.float32)
    partial = 0.0
    cols = weight_out.shape[1]
    heads = cols // HEAD_DIM
    for which in range(2):
        wait(which)
        whole = dot(low, weight[which]) + proj_bias[which : which + 1, :]
        turned = turn(whole[:, : 2 * cols], straight[...], right[...], left[...])
        turned = turned.astype(jnp.bfloat16)
        query, key = turned[:, :cols], turned[:, cols:]
        value = whole[:, 2 * cols :].astype(jnp.bfloat16)
        start = 3 * cols * which
        proj[:, start : start + 2 * cols] = turned
        proj[:, start + 2 * cols : start + 3 * cols] = value
        joined = jnp.zeros(query.shape, jnp.float32)
        for head in range(heads):
            mask = head_mask(head, query.shape)
            scores = head_scores(query, key, mask, allowed)
            highest = jnp.max(scores, -1, keepdims=True)
            powers = jnp.exp(scores - highest)
            total = jnp.sum(powers, -1, keepdims=True)
            probs = (powers * (1.0 / total)).astype(jnp.bfloat16)
            joined = jnp.where(mask, dot(probs, value), joined)
            logs = jnp.where(lane == heads * which + head, highest + jnp.log(total), logs)
        low_joined = joined.astype(jnp.bfloat16)
        attended[:, cols * which : cols * (which + 1)] = low_joined
        partial += dot(low_joined, weight_out[which])
    lse[...] = logs
    put_slot(step, partial, outs[4:])


def backward_kernel(*refs):
    slots, tokens, refs = refs[:2], refs[2:4], refs[4:]
    docs_col, docs_row, straight, right, left, proj, lse, attended, sums_in, out_in = refs[:10]
    weights = [refs[10:12], refs[12:14]]
    outs, (place, inputs, weight, weight_out, sems) = refs[-10:-5], refs[-5:]
    dproj, sums, out_sum = outs[:3]
    step = pl.program_id(0)
    wait = loader(step, weights, [weight, weight_out], sems)
    pick_slot(step, slots, place)
    pick_slot(step, tokens, inputs)

    @pl.when(step == 0)
    def _():
        sums[...] = sums_in[...]
        out_sum[...] = out_in[...]

    grad = place[...]
    out_sum[...] += contract_first(attended[...], grad)
    cols = weight_out.shape[1]
    heads = cols // HEAD_DIM
    allowed = visible(docs_col[0], docs_row[0])
    width = grad.shape[1]
    dnorm = 0.0
    for which in range(2):
        wait(which)
        datt = contract_last(grad, weight_out[which]).astype(jnp.bfloat16)
        start = 3 * cols * which
        query, key, value = (
            proj[:, start + i * cols : start + (i + 1) * cols] for i in range(3)
        )
        dquery = jnp.zeros(query.shape, jnp.float32)
        dkey, dvalue = dquery, dquery
        for head in range(heads):
            mask = head_mask(head, query.shape)
            scores = head_scores(query, key, mask, allowed)
            place_of = heads * which + head
            probs = jnp.exp(scores - lse[:, place_of : place_of + 1])
            dvalue = jnp.where(mask, contract_first(probs.astype(jnp.bfloat16), datt), dvalue)
            dprobs = contract_last(jnp.where(mask, datt, jnp.zeros_like(datt)), value)
            inner = jnp.sum(probs * dprobs, -1, keepdims=True)
            dscores = (0.125 * probs * (dprobs - inner)).astype(jnp.bfloat16)
            dquery = jnp.where(mask, dot(dscores, key), dquery)
            dkey = jnp.where(mask, contract_first(dscores, query), dkey)
        turned = turn(
            jnp.concatenate([dquery, dkey], 1), straight[...], -right[...], -left[...]
        )
        low = jnp.concatenate([turned, dvalue], 1).astype(jnp.bfloat16)
        dproj[:, start : start + 3 * cols] = low
        dnorm += contract_last(low, weight[which])
        start += 2 * width
        sums[:, start : start + 3 * cols] += jnp.sum(low.astype(jnp.float32), 0, keepdims=True)
    put_slot(step, dnorm, outs[3:])
    values = inputs[...].astype(jnp.float32)
    centered = values - jnp.mean(values, -1, keepdims=True)
    unit = centered * lax.rsqrt(jnp.mean(centered * centered, -1, keepdims=True) + 1e-05)
    sums[:, :width] += jnp.sum(dnorm * unit, 0, keepdims=True)
    sums[:, width : 2 * width] += jnp.sum(dnorm, 0, keepdims=True)


def fixed(shape):
    return pl.BlockSpec(shape, lambda i: (0,) * len(shape))


def moving(shape, first):
    return pl.BlockSpec(shape, lambda i: (first + i,) + (0,) * (len(shape) - 1))


def anywhere(count):
    return [pl.BlockSpec(memory_space=pl.ANY)] * count


def run_kernel(
    kernel, name, blocks, inputs, in_specs, shapes, out_specs, scratch, aliases, later=()
):
    given, used = len(later), kernel
    if given:

        def used(*refs):
            kernel(*refs[given:])

    aliases = {k + given: v for k, v in aliases.items()}
    return pl.pallas_call(
        used,
        grid=(blocks,),
        out_shape=shapes,
        in_specs=anywhere(given) + in_specs,
        out_specs=out_specs,
        scratch_shapes=scratch,
        input_output_aliases=aliases,
        compiler_params=pltpu.CompilerParams(vmem_limit_bytes=VMEM_BYTES),
        cost_estimate=COST,
        name=name,
    )(*later, *inputs)


def after(value, *others):
    return pl.pallas_call(
        lambda *refs: None,
        out_shape=jax.ShapeDtypeStruct(value.shape, value.dtype),
        in_specs=anywhere(1 + len(others)),
        out_specs=pl.BlockSpec(memory_space=pl.ANY),
        input_output_aliases={0: 0},
        cost_estimate=COST,
        name="after",
    )(value, *others)


def part_types(first):
    return jnp.bfloat16 if first else jnp.float32


def attention_forward(first, slots, vectors, weights, docs, tables, carried, later=()):
    length, width = slots[0].shape
    cols = weights[0][1].shape[0]
    shape = jax.ShapeDtypeStruct
    shapes = [
        shape((4 * length, width), jnp.bfloat16),
        shape((4 * length, 6 * cols), jnp.bfloat16),
        shape((4 * length, 128), jnp.float32),
        shape((4 * length, 2 * cols), jnp.bfloat16),
    ] + [shape((length, width), part_types(first))] * 2
    inputs = [*slots, *vectors, *docs, *tables, *weights[0], *weights[1], *carried]
    in_specs = (
        [fixed((length, width))] * 2
        + [fixed(v.shape) for v in vectors]
        + [moving((1, length, 1), first), moving((1, 1, length), first)]
        + [moving((length, 128), first)] * 3
        + anywhere(4 + len(carried))
    )
    out_specs = [moving((length, s.shape[1]), first) for s in shapes[:4]]
    out_specs += [fixed((length, width))] * 2
    scratch = [
        pltpu.VMEM((length, width), jnp.bfloat16),
        pltpu.VMEM((2,) + weights[0][0].shape, jnp.bfloat16),
        pltpu.VMEM((2,) + weights[0][1].shape, jnp.bfloat16),
        pltpu.SemaphoreType.DMA((2, 2)),
    ]
    aliases = {len(inputs) - len(carried) + i: i for i in range(len(carried))}

    def kernel(*refs):
        forward_kernel(first, *refs)

    return run_kernel(
        kernel,
        "attention_forward",
        2,
        inputs,
        in_specs,
        shapes,
        out_specs,
        scratch,
        aliases,
        later,
    )


def attention_backward(
    first, slots, tokens, weights, docs, tables, kept, sums, carried, later=()
):
    length, width = slots[0].shape
    cols = weights[0][1].shape[0]
    shape = jax.ShapeDtypeStruct
    shapes = (
        [shape((4 * length, 6 * cols), jnp.bfloat16)]
        + [shape(s.shape, jnp.float32) for s in sums]
        + [shape((length, width), part_types(first))] * 2
    )
    inputs = [*slots, *tokens, *docs, *tables, *kept, *sums, *weights[0], *weights[1], *carried]
    in_specs = (
        [fixed((length, width))] * 4
        + [moving((1, length, 1), first), moving((1, 1, length), first)]
        + [moving((length, 128), first)] * 3
        + [moving((length, k.shape[1]), first) for k in kept]
        + [fixed(s.shape) for s in sums]
        + anywhere(4 + len(carried))
    )
    out_specs = (
        [moving((length, 6 * cols), first)]
        + [fixed(s.shape) for s in sums]
        + [fixed((length, width))] * 2
    )
    scratch = [pltpu.VMEM((length, width), jnp.bfloat16)] * 2 + [
        pltpu.VMEM((2,) + weights[0][0].shape, jnp.bfloat16),
        pltpu.VMEM((2,) + weights[0][1].shape, jnp.bfloat16),
        pltpu.SemaphoreType.DMA((2, 2)),
    ]
    aliases = {len(inputs) - len(carried): 0} if first else {}
    return run_kernel(
        backward_kernel,
        "attention_backward",
        2,
        inputs,
        in_specs,
        shapes,
        out_specs,
        scratch,
        aliases,
        later,
    )


def last_tile(values, start):
    tile = values[:, start:]
    return tile, pltpu.roll(tile, HEAD_DIM, 1)


def hidden_kernel(*refs):
    slots, weights, refs = refs[:4], refs[4:6], refs[6:]
    raw, joined, *mixed, place, weight, sems = refs
    step = pl.program_id(0)
    wait = loader(step, [weights[:1], weights[1:]], [weight], sems)
    pick_slot(step, slots, place)
    joined[...] = place[...]
    cols = weight.shape[2]
    for which in range(2):
        wait(which)
        out = mixed[which]
        hidden = out.shape[1]
        main = hidden // 128 * 128
        both = dot(place[...], weight[which])
        raw[:, which * cols : (which + 1) * cols] = both
        gate, up = both[:, :main], both[:, main : 2 * main]
        out[:, :main] = (gate * jax.nn.sigmoid(gate) * up).astype(jnp.bfloat16)
        if main < hidden:
            gate, up = last_tile(both, 2 * main)
            rest = (gate * jax.nn.sigmoid(gate) * up).astype(jnp.bfloat16)
            out[:, main:] = rest[:, : hidden - main]


def hidden_back_kernel(grad_out, raw, *refs):
    weights = [refs[0:2], refs[2:4]]
    grads, outs, (weight, weight_down, sems) = refs[-7:-5], refs[-5:-3], refs[-3:]
    step = pl.program_id(0)
    wait = loader(step, weights, [weight, weight_down], sems)
    cols, hidden = weight.shape[2], weight_down.shape[1]
    main = hidden // 128 * 128

    def gradients(gate, up, dm):
        sig = jax.nn.sigmoid(gate)
        return dm * up * sig * (1.0 + gate * (1.0 - sig)), dm * gate * sig

    partial = 0.0
    for which in range(2):
        wait(which)
        dmixed = contract_last(grad_out[...], weight_down[which])
        both = raw[:, which * cols : (which + 1) * cols]
        pieces = list(gradients(both[:, :main], both[:, main : 2 * main], dmixed[:, :main]))
        if main < hidden:
            gate, up = last_tile(both, 2 * main)
            rest = dmixed[:, main:]
            dgate, dup = gradients(gate, up, jnp.concatenate([rest, rest], 1))
            lane = lax.broadcasted_iota(jnp.int32, dgate.shape, 1)
            pieces.append(jnp.where(lane < HEAD_DIM, dgate, pltpu.roll(dup, HEAD_DIM, 1)))
        low = jnp.concatenate(pieces, 1).astype(jnp.bfloat16)
        grads[which][...] = low
        partial += contract_last(low, weight[which])
    put_slot(step, partial, outs)


def mlp_forward(slots, weights):
    length, width = slots[0].shape
    both = weights[0].shape[1]
    shape = jax.ShapeDtypeStruct
    shapes = [
        shape((4 * length, 2 * both), jnp.float32),
        shape((4 * length, width), jnp.bfloat16),
    ] + [shape((4 * length, both // 2), jnp.bfloat16)] * 2
    scratch = [
        pltpu.VMEM((length, width), jnp.bfloat16),
        pltpu.VMEM((2,) + weights[0].shape, jnp.bfloat16),
        pltpu.SemaphoreType.DMA((2, 1)),
    ]
    return run_kernel(
        hidden_kernel,
        "mlp_forward",
        4,
        [*slots, *weights],
        [fixed((length, width))] * 4 + anywhere(2),
        shapes,
        [moving((length, s.shape[1]), 0) for s in shapes],
        scratch,
        {},
    )


def mlp_backward(first, grad_out, raw, weights, carried, later=()):
    length, width = grad_out.shape[0] // 4, grad_out.shape[1]
    both = weights[0][0].shape[1]
    shape = jax.ShapeDtypeStruct
    shapes = [shape((4 * length, both), jnp.bfloat16)] * 2
    shapes += [shape((length, width), part_types(first))] * 2
    inputs = [grad_out, raw, *weights[0], *weights[1], *carried]
    scratch = [
        pltpu.VMEM((2,) + weights[0][0].shape, jnp.bfloat16),
        pltpu.VMEM((2,) + weights[0][1].shape, jnp.bfloat16),
        pltpu.SemaphoreType.DMA((2, 2)),
    ]
    return run_kernel(
        hidden_back_kernel,
        "mlp_backward",
        2,
        inputs,
        [moving((length, width), first), moving((length, 2 * both), first)]
        + anywhere(4 + len(carried)),
        shapes,
        [moving((length, both), first)] * 2 + [fixed((length, width))] * 2,
        scratch,
        {6 + i: i for i in range(len(carried))},
        later,
    )


def join_kernel(*refs):
    pick_slot(pl.program_id(0), refs[:-1], refs[-1])


def join(parts):
    length, width = parts[0].shape
    return run_kernel(
        join_kernel,
        "join",
        len(parts),
        parts,
        [fixed((length, width))] * len(parts),
        jax.ShapeDtypeStruct((len(parts) * length, width), parts[0].dtype),
        moving((length, width), 0),
        [],
        {},
    )


def gather_z(values):
    return lax.all_gather(values, "z", axis=0, tiled=True)


def scatter_z(values):
    return lax.psum_scatter(values, "z", scatter_dimension=0, tiled=True)


def per_device(
    tokens,
    doc_ids,
    cotangent,
    ln1_gain,
    ln1_bias,
    w_qkv,
    b_qkv,
    w_out,
    ln2_gain,
    ln2_bias,
    w_gate,
    w_up,
    w_down,
):
    x_index, z_index = lax.axis_index("x"), lax.axis_index("z")
    y_index, c_index = lax.axis_index("y"), lax.axis_index("c")
    yc_index = 2 * y_index + c_index
    planes = lax.axis_size("z")
    shards = 4 * planes
    rows = w_qkv.shape[0]
    width = rows * shards
    hidden_dim = w_gate.shape[1]
    piece = hidden_dim // (2 * shards)
    mlp = piece * planes
    head_cols = width // 8
    spread = rows % (2 * HEAD_DIM) == 0
    groups = planes if spread else 1
    unit = head_cols // groups
    length = tokens.shape[0]

    def pick_x(values, axis):
        return lax.dynamic_index_in_dim(values, x_index, axis, keepdims=False)

    def pick_yc(values, axis):
        return lax.dynamic_index_in_dim(values, yc_index, axis, keepdims=False)

    def columns(weight, outer, size):
        view = pick_x(weight.reshape(rows, outer, 4, 2, size), 3)
        return [view[:, :, t].reshape(rows, outer * size) for t in range(4)]

    def rows_of_plane(blocks):
        return jnp.concatenate(exchange(blocks, y_index, c_index), 0)

    main = mlp // 128 * 128

    def pair(gate, up):
        return jnp.concatenate([gate[:, :main], up[:, :main], gate[:, main:], up[:, main:]], 1)

    def unpair(both):
        rest = both[..., 2 * main :]
        return (
            jnp.concatenate([both[..., :main], rest[..., : mlp - main]], -1),
            jnp.concatenate([both[..., main : 2 * main], rest[..., mlp - main :]], -1),
        )

    vectors = gather_small(
        jnp.concatenate([ln1_gain, ln1_bias, ln2_gain, ln2_bias, b_qkv]), planes
    )
    block_qkv = rows_of_plane(columns(w_qkv, 3 * groups, unit))
    full_qkv = gather_z(after(block_qkv, vectors))
    if spread:
        full_out = gather_rows(pick_x(w_out.reshape(2, rows // 2, width), 0), planes)
    else:
        full_out = lax.all_gather(w_out, ("z", "y", "c"), axis=0, tiled=True)
        full_out = pick_x(pick_yc(full_out.reshape(4, 2, unit, width), 0), 0)
    block_both = rows_of_plane(
        [
            pair(gate, up)
            for gate, up in zip(columns(w_gate, planes, piece), columns(w_up, planes, piece))
        ]
    )
    full_both = gather_z(block_both)
    full_down = gather_z(pick_x(w_down.reshape(2, piece, width), 0))

    vectors = vectors.astype(jnp.float32)
    gain_one, bias_one, gain_two, bias_two = (
        vectors[:, i * rows : (i + 1) * rows].reshape(width) for i in range(4)
    )
    bias_qkv = vectors[:, 4 * rows :].reshape(3 * groups, 4, 2, unit)
    bias_qkv = pick_x(bias_qkv, 2)
    bias_qkv = jnp.stack(
        [
            lax.dynamic_index_in_dim(bias_qkv, yc_index ^ k, 1, keepdims=False).reshape(-1)
            for k in range(2)
        ]
    )

    docs = jnp.stack(plane_gather(doc_ids))
    token_slots = plane_gather(after(tokens, block_qkv))
    all_cot = join(plane_gather(after(cotangent, token_slots[3])))

    indices = jnp.arange(length, dtype=jnp.int32)
    same_doc = docs[:, :, None] == docs[:, None, :]
    first_row = jnp.min(jnp.where(same_doc, indices[None, None, :], length), axis=2)
    tables = spread_rotary((indices[None] - first_row).reshape(-1))
    docs = (docs[:, :, None], docs[:, None, :])

    norm_vectors = (gain_one[None], bias_one[None], bias_qkv)
    full_qkv = after(
        full_qkv, full_out, block_both, token_slots[3], *tables, *docs, *norm_vectors
    )
    weights = list(zip(with_sibling(full_qkv), with_sibling(full_out)))
    *carried, side_part, far_part = attention_forward(
        2, token_slots[2:], norm_vectors, weights, docs, tables, ()
    )
    normed_low, proj, lse, attended_low, own_part, near_part = attention_forward(
        0, token_slots[:2], norm_vectors, weights, docs, tables, carried, (all_cot,)
    )
    inputs = tokens.astype(jnp.float32)
    hidden = inputs + plane_sum(own_part, near_part, side_part, far_part)[1]()
    normed_two, unit_two, scale_two = layer_norm(hidden, gain_two, bias_two)
    two_slots = plane_gather(normed_two.astype(jnp.bfloat16))
    both_weights = with_sibling(after(full_both, two_slots[1]))
    raw, two_low, *mixed = mlp_forward(two_slots, both_weights)
    down_weights = with_sibling(after(full_down, raw))
    mlp_weights = list(zip(both_weights, down_weights))

    def chip_grad(left, right):
        there = swap(contract_first(left[1], right[1]).astype(jnp.bfloat16), SIBLING)
        here = contract_first(left[0], right[0])
        return (here + there.astype(jnp.float32)).astype(jnp.bfloat16)

    down_grad = chip_grad(mixed, [all_cot] * 2)
    down_sum = scatter_z(down_grad)
    *carried, side_part, far_part = mlp_backward(2, all_cot, raw, mlp_weights, (), (down_grad,))
    *both_grads, own_part, near_part = mlp_backward(0, all_cot, raw, mlp_weights, carried)
    near_low, finish = plane_sum(own_part, near_part, side_part, far_part)
    grad_norm_two = finish()
    two_late = after(two_low, near_low)
    there = swap(contract_first(two_late, both_grads[1]).astype(jnp.bfloat16), SIBLING)
    mixed = [after(m, near_low) for m in mixed]
    down_part = dot(mixed[0], down_weights[0]) + dot(mixed[1], down_weights[1])
    down_part = down_part.reshape(4, length, width)
    down_low = down_part[2:].astype(jnp.bfloat16)
    _, finish = plane_sum(down_part[0], down_part[1], down_low[0], down_low[1])
    activations = (hidden + finish()).astype(jnp.bfloat16)
    grad_gain_two = jnp.sum(grad_norm_two * unit_two, 0)
    grad_bias_two = jnp.sum(grad_norm_two, 0)
    grad_hidden = cotangent.astype(jnp.float32) + norm_back(
        grad_norm_two, unit_two, scale_two, gain_two
    )
    hidden_low = after(grad_hidden.astype(jnp.bfloat16), down_sum)
    here = contract_first(after(two_late, hidden_low), both_grads[0])
    both_grad = (here + there.astype(jnp.float32)).astype(jnp.bfloat16)
    both_sum = scatter_z(both_grad)
    hidden_slots = plane_gather(hidden_low)
    kept = (proj, lse, attended_low)
    sums = [
        jnp.zeros((1, 2 * width + 6 * head_cols), jnp.float32),
        jnp.zeros((2 * head_cols, width), jnp.float32),
    ]
    grad_proj_low, *sums, own_part, near_part = attention_backward(
        0, hidden_slots[:2], token_slots[:2], weights, docs, tables, kept, sums, (), (both_grad,)
    )
    grad_proj_low, vector_sums, out_sum, side_part, far_part = attention_backward(
        2, hidden_slots[2:], token_slots[2:], weights, docs, tables, kept, sums, (grad_proj_low,)
    )
    qkv_grad = chip_grad(
        [normed_low] * 2,
        [grad_proj_low[:, : 3 * head_cols], grad_proj_low[:, 3 * head_cols :]],
    )
    qkv_sum = scatter_z(after(qkv_grad, both_sum))
    out_there = swap(out_sum[head_cols:].astype(jnp.bfloat16), SIBLING)
    out_part = (out_sum[:head_cols] + out_there.astype(jnp.float32)).astype(jnp.bfloat16)
    placed = jnp.zeros((3 * groups, 4, 2, unit), jnp.float32)
    for k in range(2):
        piece_sum = vector_sums[0, 2 * width + 3 * head_cols * k :][: 3 * head_cols]
        placed = lax.dynamic_update_slice(
            placed,
            piece_sum.reshape(3 * groups, 1, 1, unit),
            (0, yc_index ^ k, x_index, 0),
        )
    grad_norm_one = plane_sum(own_part, near_part, side_part, far_part)[1]()
    _, unit_one, scale_one = layer_norm(inputs, gain_one, bias_one)
    grad_gain_one, grad_bias_one = vector_sums[0, :width], vector_sums[0, width : 2 * width]
    d_tokens = grad_hidden + norm_back(grad_norm_one, unit_one, scale_one, gain_one)

    sums = sum_small(
        jnp.concatenate(
            [
                grad_gain_one,
                grad_bias_one,
                grad_gain_two,
                grad_bias_two,
                placed.reshape(3 * width),
            ]
        ),
        planes,
    )
    shard_index = 4 * z_index + yc_index
    small = [
        lax.dynamic_slice_in_dim(sums[i * width : (i + 1) * width], shard_index * rows, rows)
        for i in range(4)
    ]
    owned_bqkv = lax.dynamic_slice_in_dim(sums[4 * width :], shard_index * 3 * rows, 3 * rows)

    def whole_rows(half):
        other = swap(half, ACROSS_X)
        odd = x_index == 1
        return jnp.concatenate(
            [jnp.where(odd, other, half), jnp.where(odd, half, other)], 0
        ).astype(jnp.float32)

    if spread:
        owned_out = whole_rows(scatter_z(after(out_part, qkv_sum)))
    else:
        placed_out = lax.dynamic_update_slice(
            jnp.zeros((4, 2, unit, width), jnp.bfloat16),
            out_part[None, None],
            (yc_index, x_index, 0, 0),
        )
        owned_out = lax.psum_scatter(
            placed_out.reshape(width, width), ("z", "y", "c"), scatter_dimension=0, tiled=True
        )
        owned_out = lax.psum(owned_out, "x").astype(jnp.float32)

    def whole_columns(summed):
        blocks = summed.reshape(4, rows, summed.shape[1])
        half = jnp.stack(exchange([blocks[t] for t in range(4)], y_index, c_index))
        other = swap(half, ACROSS_X)
        odd = x_index == 1
        return jnp.stack([jnp.where(odd, other, half), jnp.where(odd, half, other)])

    def in_order(both, outer, size):
        both = both.reshape(2, 4, rows, outer, size)
        return both.transpose(2, 3, 1, 0, 4).reshape(rows, -1).astype(jnp.float32)

    owned_qkv = in_order(whole_columns(qkv_sum), 3 * groups, unit)
    owned_gate, owned_up = (
        in_order(half, planes, piece) for half in unpair(whole_columns(both_sum))
    )

    return (
        activations,
        d_tokens,
        small[0],
        small[1],
        owned_qkv,
        owned_bqkv,
        owned_out,
        small[2],
        small[3],
        owned_gate,
        owned_up,
        whole_rows(down_sum),
    )


def solution(mesh):
    reps, shards = mesh.shape["rep"], mesh.shape["shard"]
    grid = Mesh(mesh.devices.reshape(reps, shards // 4, 2, 2), EVERY)
    tokens, rows, vector = P(EVERY, None), P(("z", "y", "c"), None), P(("z", "y", "c"))
    return jax.shard_map(
        per_device,
        mesh=grid,
        in_specs=(
            tokens,
            P(EVERY),
            tokens,
            vector,
            vector,
            rows,
            vector,
            rows,
            vector,
            vector,
            rows,
            rows,
            rows,
        ),
        out_specs=(
            tokens,
            tokens,
            vector,
            vector,
            rows,
            vector,
            rows,
            vector,
            vector,
            rows,
            rows,
            rows,
        ),
        check_vma=False,
    )
```

```python
import jax
import jax.numpy as jnp
from jax import lax
from jax.experimental import pallas as pl
from jax.experimental.pallas import tpu as pltpu
from jax.sharding import Mesh, PartitionSpec as P

HEAD_DIM = 64
ROT = 16
PLANE = ("x", "y", "c")
EVERY = ("x", "z", "y", "c")
SIBLING = (1, 1)
FIRST = (4, 2)
SECOND = (2, 4)
ACROSS_X = (4, 4)
ACROSS_Y = (2, 2)
ACROSS_YC = (3, 3)
VMEM_BYTES = 48 << 20
EXTRA_ROWS = 16
MICROSECONDS = {
    "attention_forward": 15,
    "attention_backward": 18,
    "mlp_forward": 21,
    "mlp_backward": 21,
    "mlp_output": 13,
    "token_product": 14,
    "norm_forward": 5,
    "norm_backward": 5,
    "spread_columns": 4,
    "pick_columns": 3,
    "place_blocks": 1,
    "split_blocks": 1,
    "unpack_vectors": 1,
    "after": 0,
}


def cost(name):
    return cost_of(MICROSECONDS[name])


def cost_of(us):
    flops = us * 1_150_000_000 + 1_000_000
    return pl.CostEstimate(flops=flops, bytes_accessed=1 << 10, transcendentals=0)


def swap(values, masks):
    pairs = [(i, i ^ masks[i & 1]) for i in range(8)]
    return lax.ppermute(values, PLANE, pairs)


def plane_gather(values):
    side = swap(values, SECOND)
    near = after(swap(values, FIRST), side)
    return [values, near, side, swap(near, SECOND)]


def plane_sum(own, near, side, far, later=()):
    far = swap(far, SECOND)
    side = swap(side, SECOND)
    near = after((near + far.astype(jnp.float32)).astype(jnp.bfloat16), side, *later)

    return near, (own, side, swap(near, FIRST))


def with_sibling(values):
    return [values, swap(values, SIBLING)]


def exchange(blocks, later=()):
    if later:
        blocks = [blocks[0]] + [after(block, *later) for block in blocks[1:]]
    blocks, masks = list(blocks), (None, SIBLING, ACROSS_Y, ACROSS_YC)
    return blocks[:1] + [swap(blocks[k], masks[k]) for k in range(1, 4)]


def meet(values, axis, bit, size):
    return lax.ppermute(values, axis, [(i, i ^ bit) for i in range(size)])


def gather_direct(block, axis, size):
    parts = [block] + [meet(block, axis, k, size) for k in range(1, size)]
    return place_blocks(parts, lax.axis_index(axis))


def layer_norm(values, gain_vec, bias_vec):
    average = jnp.mean(values, -1, keepdims=True)
    centered = values - average
    recip_std = lax.rsqrt(jnp.mean(centered * centered, -1, keepdims=True) + 1e-05)
    unit_vals = centered * recip_std
    return (unit_vals * gain_vec + bias_vec, unit_vals, recip_std)


def norm_back(grad_in, unit_vals, recip_std, gain_vec):
    scaled = grad_in * gain_vec
    return recip_std * (
        scaled
        - jnp.mean(scaled, -1, keepdims=True)
        - unit_vals * jnp.mean(scaled * unit_vals, -1, keepdims=True)
    )


def dot(left, right):
    return jnp.dot(left, right, preferred_element_type=jnp.float32)


def contract_last(left, right):
    return lax.dot_general(
        left, right, (((1,), (1,)), ((), ())), preferred_element_type=jnp.float32
    )


def contract_first(left, right):
    return lax.dot_general(
        left, right, (((0,), (0,)), ((), ())), preferred_element_type=jnp.float32
    )


def spread_rotary(positions):
    half_rot = ROT // 2
    frequency = 10000.0 ** (-(jnp.arange(half_rot, dtype=jnp.float32) * 2.0 / ROT))
    lane = jnp.arange(2 * HEAD_DIM) % HEAD_DIM
    frequency = jnp.where(lane < ROT, jnp.tile(frequency, 2 * HEAD_DIM // half_rot), 0.0)
    angles = positions.astype(jnp.float32)[:, None] * frequency
    sine = jnp.sin(angles)
    from_right = jnp.where(lane < half_rot, -sine, 0.0)
    from_left = jnp.where(lane < half_rot, 0.0, sine)
    return jnp.concatenate([jnp.cos(angles), from_right, from_left], 1)


def turn(values, table, direction):
    cols, lanes = values.shape[1], 2 * HEAD_DIM
    times = cols // lanes
    wide = [jnp.concatenate([table[:, k * lanes : (k + 1) * lanes]] * times, 1) for k in range(3)]
    half_rot = ROT // 2
    from_right = pltpu.roll(values, cols - half_rot, 1) * wide[1]
    from_left = pltpu.roll(values, half_rot, 1) * wide[2]
    return values * wide[0] + direction * (from_right + from_left)


def head_mask(head, shape):
    lane = lax.broadcasted_iota(jnp.int32, shape, 1)
    return (lane >= head * HEAD_DIM) & (lane < (head + 1) * HEAD_DIM)


def visible(docs_col, docs_row):
    shape = (docs_col.shape[0], docs_row.shape[1])
    row = lax.broadcasted_iota(jnp.int32, shape, 0)
    col = lax.broadcasted_iota(jnp.int32, shape, 1)
    return (docs_col == docs_row) & (col <= row)


def by_head(values):
    heads = values.shape[1] // HEAD_DIM
    zero = jnp.zeros_like(values)
    return jnp.concatenate(
        [jnp.where(head_mask(head, values.shape), values, zero) for head in range(heads)], 0
    )


def join_heads(stacked):
    heads = stacked.shape[1] // HEAD_DIM
    rows = stacked.shape[0] // heads
    joined = stacked[:rows]
    for head in range(1, heads):
        part = stacked[head * rows : (head + 1) * rows]
        joined = jnp.where(head_mask(head, part.shape), part, joined)
    return joined


def head_scores(query_heads, key, allowed):
    return jnp.where(allowed, contract_last(query_heads, key) * 0.125, -1e30)


def pick_slot(step, slots, place):
    for k, slot in enumerate(slots):

        @pl.when(step == k)
        def _(slot=slot):
            place[...] = slot[...]


def put_slot(step, value, slots):
    for k, slot in enumerate(slots):

        @pl.when(step == k)
        def _(slot=slot):
            slot[...] = value.astype(slot.dtype)


def loader(step, sources, places, sems):
    def copies(which):
        return [
            pltpu.make_async_copy(sources[which][k], places[k].at[which], sems.at[which, k])
            for k in range(len(places))
        ]

    @pl.when(step == 0)
    def _():
        for which in range(2):
            for copy in copies(which):
                copy.start()

    def wait(which):
        @pl.when(step == 0)
        def _():
            for copy in copies(which):
                copy.wait()

    return wait


def forward_kernel(first, *refs):
    slots, refs = refs[:2], refs[2:]
    vectors, docs_col, docs_row, table = refs[:4]
    weights = [refs[4:6], refs[6:8]]
    outs, (place, weight, weight_out, sems) = refs[-10:-4], refs[-4:]
    normed, proj, lse, attended = outs[:4]
    step = pl.program_id(0)
    wait = loader(step, weights, [weight, weight_out], sems)
    pick_slot(step, slots, place)
    width = normed.shape[1]
    gain, bias = vectors[:1, :width], vectors[:1, width : 2 * width]
    values, _, _ = layer_norm(place[...].astype(jnp.float32), gain, bias)
    low = values.astype(jnp.bfloat16)
    normed[...] = low
    allowed = visible(docs_col[0], docs_row[0])
    allowed = jnp.concatenate([allowed] * (weight_out.shape[1] // HEAD_DIM), 0)
    lane = lax.broadcasted_iota(jnp.int32, lse.shape, 1)
    logs = jnp.zeros(lse.shape, jnp.float32)
    partial = 0.0
    cols = weight_out.shape[1]
    heads = cols // HEAD_DIM
    for which in range(2):
        wait(which)
        start = 4 * width + 3 * cols * which
        whole = dot(low, weight[which]) + vectors[:1, start : start + 3 * cols]
        turned = turn(whole[:, : 2 * cols], table[...], 1.0)
        turned = turned.astype(jnp.bfloat16)
        query, key = turned[:, :cols], turned[:, cols:]
        value = whole[:, 2 * cols :].astype(jnp.bfloat16)
        start = 3 * cols * which
        proj[:, start : start + 2 * cols] = turned
        proj[:, start + 2 * cols : start + 3 * cols] = value
        scores = head_scores(by_head(query), key, allowed)
        highest = jnp.max(scores, -1, keepdims=True)
        powers = jnp.exp(scores - highest)
        total = jnp.sum(powers, -1, keepdims=True)
        probs = (powers * (1.0 / total)).astype(jnp.bfloat16)
        joined = join_heads(dot(probs, value))
        log_total = highest + jnp.log(total)
        rows = query.shape[0]
        for head in range(heads):
            part = log_total[head * rows : (head + 1) * rows]
            logs = jnp.where(lane == heads * which + head, part, logs)
        low_joined = joined.astype(jnp.bfloat16)
        attended[:, cols * which : cols * (which + 1)] = low_joined
        partial += dot(low_joined, weight_out[which])
    lse[...] = logs
    put_slot(step, partial, outs[4:])


def backward_kernel(count, *refs):
    slots, tokens, refs = refs[:count], refs[count : 2 * count], refs[2 * count :]
    docs_col, docs_row, table, proj, lse, sums_in = refs[:6]
    weights = [refs[6:8], refs[8:10]]
    outs, (place, inputs, weight, weight_out, sems) = refs[-7 - 2 * count : -5], refs[-5:]
    dproj, sums, dproj_there = outs[0], outs[1], outs[2 : 2 + count]
    step = pl.program_id(0)
    wait = loader(step, weights, [weight, weight_out], sems)
    pick_slot(step, slots, place)
    pick_slot(step, tokens, inputs)

    @pl.when(step == 0)
    def _():
        sums[...] = sums_in[...]

    grad = place[...]
    cols = weight_out.shape[1]
    heads = cols // HEAD_DIM
    allowed = visible(docs_col[0], docs_row[0])
    allowed = jnp.concatenate([allowed] * heads, 0)
    width = grad.shape[1]
    dnorm = 0.0
    for which in range(2):
        wait(which)
        datt = contract_last(grad, weight_out[which]).astype(jnp.bfloat16)
        start = 3 * cols * which
        query, key, value = (
            proj[:, start + i * cols : start + (i + 1) * cols] for i in range(3)
        )
        query_heads, datt_heads = by_head(query), by_head(datt)
        scores = head_scores(query_heads, key, allowed)
        log_total = jnp.concatenate(
            [lse[:, heads * which + head : heads * which + head + 1] for head in range(heads)], 0
        )
        probs = jnp.exp(scores - log_total)
        dvalue = contract_first(probs.astype(jnp.bfloat16), datt_heads)
        dprobs = contract_last(datt_heads, value)
        inner = jnp.sum(probs * dprobs, -1, keepdims=True)
        dscores = (0.125 * probs * (dprobs - inner)).astype(jnp.bfloat16)
        dquery = join_heads(dot(dscores, key))
        dkey = contract_first(dscores, query_heads)
        turned = turn(jnp.concatenate([dquery, dkey], 1), table[...], -1.0)
        low = jnp.concatenate([turned, dvalue], 1).astype(jnp.bfloat16)
        if which == 0:
            dproj[...] = low
        else:
            put_slot(step, low, dproj_there)
        dnorm += contract_last(low, weight[which])
        start += 2 * width
        sums[:, start : start + 3 * cols] += jnp.sum(low.astype(jnp.float32), 0, keepdims=True)
    put_slot(step, dnorm, outs[2 + count :])
    values = inputs[...].astype(jnp.float32)
    centered = values - jnp.mean(values, -1, keepdims=True)
    unit = centered * lax.rsqrt(jnp.mean(centered * centered, -1, keepdims=True) + 1e-05)
    sums[:, :width] += jnp.sum(dnorm * unit, 0, keepdims=True)
    sums[:, width : 2 * width] += jnp.sum(dnorm, 0, keepdims=True)


def standardized(values):
    centered = values - jnp.mean(values, -1, keepdims=True)
    recip_std = lax.rsqrt(jnp.mean(centered * centered, -1, keepdims=True) + 1e-05)
    return centered * recip_std, recip_std


def norm_forward(tokens, parts, vectors):
    length, width = tokens.shape
    step = length // 4

    def kernel(token_ref, own, side, near, vec, hidden, low):
        total = own[...] + side[...].astype(jnp.float32) + near[...].astype(jnp.float32)
        total += token_ref[...].astype(jnp.float32)
        hidden[...] = total
        unit, _ = standardized(total)
        gain, bias = vec[:1, 2 * width : 3 * width], vec[:1, 3 * width : 4 * width]
        low[...] = (unit * gain + bias).astype(jnp.bfloat16)

    block = moving((step, width), 0)
    return run_kernel(
        kernel,
        "norm_forward",
        4,
        [tokens, *parts, vectors],
        [block] * 4 + [fixed(vectors.shape)],
        [jax.ShapeDtypeStruct((length, width), d) for d in (jnp.float32, jnp.bfloat16)],
        [block] * 2,
        [],
        {},
    )


def norm_backward(values, straight, parts, vectors, which, with_sums, later=()):
    length, width = values.shape
    step = length // 4

    def kernel(value_ref, straight_ref, own, side, near, vec, total, *more):
        grad = own[...] + side[...].astype(jnp.float32) + near[...].astype(jnp.float32)
        unit, recip_std = standardized(value_ref[...].astype(jnp.float32))
        gain = vec[:1, 2 * which * width : (2 * which + 1) * width]
        back = norm_back(grad, unit, recip_std, gain)
        back += straight_ref[...].astype(jnp.float32)
        total[...] = back
        if with_sums:
            low, sums = more
            low[...] = back.astype(jnp.bfloat16)

            @pl.when(pl.program_id(0) == 0)
            def _():
                sums[...] = jnp.zeros_like(sums)

            sums[:, :width] += jnp.sum(grad * unit, 0, keepdims=True)
            sums[:, width:] += jnp.sum(grad, 0, keepdims=True)

    block = moving((step, width), 0)
    shape = jax.ShapeDtypeStruct
    shapes, specs = [shape((length, width), jnp.float32)], [block]
    if with_sums:
        shapes += [shape((length, width), jnp.bfloat16), shape((1, 2 * width), jnp.float32)]
        specs += [block, fixed((1, 2 * width))]
    return run_kernel(
        kernel,
        "norm_backward",
        4,
        [values, straight, *parts, vectors],
        [block] * 5 + [fixed(vectors.shape)],
        shapes,
        specs,
        [],
        {},
        later,
    )


def fixed(shape):
    return pl.BlockSpec(shape, lambda i: (0,) * len(shape))


def moving(shape, first):
    return pl.BlockSpec(shape, lambda i: (first + i,) + (0,) * (len(shape) - 1))


def anywhere(count):
    return [pl.BlockSpec(memory_space=pl.ANY)] * count


def run_kernel(
    kernel, name, blocks, inputs, in_specs, shapes, out_specs, scratch, aliases, later=(), us=None
):
    given, used = len(later), kernel
    if given:

        def used(*refs):
            kernel(*refs[given:])

    aliases = {k + given: v for k, v in aliases.items()}
    return pl.pallas_call(
        used,
        grid=(blocks,),
        out_shape=shapes,
        in_specs=anywhere(given) + in_specs,
        out_specs=out_specs,
        scratch_shapes=scratch,
        input_output_aliases=aliases,
        compiler_params=pltpu.CompilerParams(vmem_limit_bytes=VMEM_BYTES),
        cost_estimate=cost(name) if us is None else cost_of(us),
        name=name,
    )(*later, *inputs)


def after(value, *others):
    return pl.pallas_call(
        lambda *refs: None,
        out_shape=jax.ShapeDtypeStruct(value.shape, value.dtype),
        in_specs=anywhere(1 + len(others)),
        out_specs=pl.BlockSpec(memory_space=pl.ANY),
        input_output_aliases={0: 0},
        cost_estimate=cost("after"),
        name="after",
    )(value, *others)


def part_types(first):
    return jnp.bfloat16 if first >= 2 else jnp.float32


def attention_forward(first, slots, vectors, weights, docs, table, carried, later=()):
    length, width = slots[0].shape
    cols = weights[0][1].shape[0]
    shape = jax.ShapeDtypeStruct
    shapes = [
        shape((4 * length, width), jnp.bfloat16),
        shape((4 * length, 6 * cols), jnp.bfloat16),
        shape((4 * length, 128), jnp.float32),
        shape((4 * length, 2 * cols), jnp.bfloat16),
    ] + [shape((length, width), part_types(first))] * 2
    inputs = [*slots, vectors, *docs, table, *weights[0], *weights[1], *carried]
    in_specs = (
        [fixed((length, width))] * 2
        + [fixed(vectors.shape)]
        + [moving((1, length, 1), first), moving((1, 1, length), first)]
        + [moving((length, table.shape[1]), first)]
        + anywhere(4 + len(carried))
    )
    out_specs = [moving((length, s.shape[1]), first) for s in shapes[:4]]
    out_specs += [fixed((length, width))] * 2
    scratch = [
        pltpu.VMEM((length, width), jnp.bfloat16),
        pltpu.VMEM((2,) + weights[0][0].shape, jnp.bfloat16),
        pltpu.VMEM((2,) + weights[0][1].shape, jnp.bfloat16),
        pltpu.SemaphoreType.DMA((2, 2)),
    ]
    aliases = {len(inputs) - len(carried) + i: i for i in range(len(carried))}

    def kernel(*refs):
        forward_kernel(first, *refs)

    return run_kernel(
        kernel,
        "attention_forward",
        2,
        inputs,
        in_specs,
        shapes,
        out_specs,
        scratch,
        aliases,
        later,
    )


def attention_backward(
    first, slots, tokens, weights, docs, table, kept, sums, carried, later=()
):
    length, width = slots[0].shape
    cols, count = weights[0][1].shape[0], len(slots)
    shape = jax.ShapeDtypeStruct
    shapes = [shape((4 * length, 3 * cols), jnp.bfloat16), shape(sums.shape, jnp.float32)]
    shapes += [shape((length, 3 * cols), jnp.bfloat16)] * count
    shapes += [shape((length, width), part_types(first))] * count
    inputs = [*slots, *tokens, *docs, table, *kept, sums, *weights[0], *weights[1], *carried]
    in_specs = (
        [fixed((length, width))] * (2 * count)
        + [moving((1, length, 1), first), moving((1, 1, length), first)]
        + [moving((length, table.shape[1]), first)]
        + [moving((length, k.shape[1]), first) for k in kept]
        + [fixed(sums.shape)]
        + anywhere(4 + len(carried))
    )
    out_specs = [moving((length, 3 * cols), first)] + [fixed(s.shape) for s in shapes[1:]]
    scratch = [pltpu.VMEM((length, width), jnp.bfloat16)] * 2 + [
        pltpu.VMEM((2,) + weights[0][0].shape, jnp.bfloat16),
        pltpu.VMEM((2,) + weights[0][1].shape, jnp.bfloat16),
        pltpu.SemaphoreType.DMA((2, 2)),
    ]

    def kernel(*refs):
        backward_kernel(count, *refs)

    return run_kernel(
        kernel,
        "attention_backward",
        count,
        inputs,
        in_specs,
        shapes,
        out_specs,
        scratch,
        {len(inputs) - len(carried): 0} if carried else {},
        later,
    )


def token_product(pairs, rows, cols, later=(), extra=None, us=None):
    by_rows, step = rows % 512 == 0, 512
    if extra is not None:
        step = rows * EXTRA_ROWS // extra.shape[0]
    grid = (rows if by_rows else cols) // step

    def fixed_columns(length, size, window):
        return pl.BlockSpec((length, size), lambda i: (0, window))

    def step_columns(length, window):
        return pl.BlockSpec((length, step), lambda i: (0, window * grid + i))

    sides, inputs, specs = [[], []], [], []
    for pair in pairs:
        for side, (blocks, window) in enumerate(pair):
            for block in blocks:
                sides[side].append((len(inputs), block.shape[0]))
                inputs.append(block)
                if by_rows == (side == 0):
                    specs.append(step_columns(block.shape[0], window))
                else:
                    specs.append(fixed_columns(block.shape[0], (rows, cols)[side], window))
    tokens = sum(length for _, length in sides[0])
    shape, place = (rows, cols), pl.BlockSpec((step, cols), lambda i: (i, 0))
    if not by_rows:
        place = pl.BlockSpec((rows, step), lambda i: (0, i))
    if extra is not None:
        inputs, specs = inputs + [extra], specs + [moving((EXTRA_ROWS, cols), 0)]
        place = moving((step + EXTRA_ROWS, cols), 0)
        shape = (rows + extra.shape[0], cols)

    def kernel(*refs):
        out, left, right = refs[-3:]

        def fill(side, whole):
            start = 0
            for k, length in sides[side]:
                whole[start : start + length, :] = refs[k][...]
                start += length

        moved, kept = (0, 1) if by_rows else (1, 0)
        wholes = (left, right)
        fill(moved, wholes[moved])

        @pl.when(pl.program_id(0) == 0)
        def _():
            fill(kept, wholes[kept])

        total = contract_first(left[...], right[...]).astype(out.dtype)
        if extra is None:
            out[...] = total
        else:
            out[:step, :] = total
            out[step:, :] = refs[-4][...]

    left_cols, right_cols = (step, cols) if by_rows else (rows, step)
    return run_kernel(
        kernel,
        "token_product",
        grid,
        inputs,
        specs,
        jax.ShapeDtypeStruct(shape, jnp.bfloat16),
        place,
        [pltpu.VMEM((tokens, size), jnp.bfloat16) for size in (left_cols, right_cols)],
        {},
        later,
        us,
    )


def spread_columns(half, other, x_index, split, outer, size):
    blocks, rows, cols = half.shape
    width = 8 * outer * size
    outs = len(split(jnp.zeros((8, cols), jnp.float32)))
    step = min(rows, 32)

    def kernel(x_ref, half_ref, other_ref, *out_refs):
        here = x_ref[0]
        for t in range(blocks):
            mine, theirs = half_ref[t].astype(jnp.float32), other_ref[t].astype(jnp.float32)
            for x in range(2):
                columns = split(jnp.where(here == x, mine, theirs))
                for out, values in zip(out_refs, columns):
                    for k in range(outer):
                        start = ((k * blocks + t) * 2 + x) * size
                        out[:, start : start + size] = values[:, k * size : (k + 1) * size]

    block = pl.BlockSpec((blocks, step, cols), lambda i: (0, i, 0))
    return run_kernel(
        kernel,
        "spread_columns",
        rows // step,
        [scalar(x_index), half, other],
        [pl.BlockSpec(memory_space=pltpu.SMEM), block, block],
        [jax.ShapeDtypeStruct((rows, width), jnp.float32)] * outs,
        [pl.BlockSpec((step, width), lambda i: (i, 0))] * outs,
        [],
        {},
    )


def last_tile(values, start):
    tile = values[:, start:]
    return tile, pltpu.roll(tile, HEAD_DIM, 1)


def hidden_kernel(*refs):
    slots, weights, refs = refs[:4], refs[4:6], refs[6:]
    raw, mixed, mixed_there, (place, weight, sems) = refs[0], refs[1], refs[2:6], refs[6:]
    step = pl.program_id(0)
    wait = loader(step, [weights[:1], weights[1:]], [weight], sems)
    pick_slot(step, slots, place)
    cols, hidden = weight.shape[2], mixed.shape[1]
    main = hidden // 128 * 128

    def mix(gate, up):
        return (gate * jax.nn.sigmoid(gate) * up).astype(jnp.bfloat16)

    for which in range(2):
        wait(which)
        both = dot(place[...], weight[which])
        raw[:, which * cols : (which + 1) * cols] = both
        pieces = [mix(both[:, :main], both[:, main : 2 * main])]
        if main < hidden:
            pieces.append(mix(*last_tile(both, 2 * main))[:, : hidden - main])
        low = jnp.concatenate(pieces, 1)
        if which == 0:
            mixed[...] = low
        else:
            put_slot(step, low, mixed_there)


def hidden_back_kernel(*refs):
    slots, raw, refs = refs[:2], refs[2], refs[3:]
    weights = [refs[0:2], refs[2:4]]
    grads, grads_there, outs = refs[-9], refs[-8:-6], refs[-6:-4]
    grad_out, weight, weight_down, sems = refs[-4:]
    step = pl.program_id(0)
    wait = loader(step, weights, [weight, weight_down], sems)
    pick_slot(step, slots, grad_out)
    cols, hidden = weight.shape[2], weight_down.shape[1]
    main = hidden // 128 * 128

    def gradients(gate, up, dm):
        sig = jax.nn.sigmoid(gate)
        return dm * up * sig * (1.0 + gate * (1.0 - sig)), dm * gate * sig

    partial = 0.0
    for which in range(2):
        wait(which)
        dmixed = contract_last(grad_out[...], weight_down[which])
        both = raw[:, which * cols : (which + 1) * cols]
        pieces = list(gradients(both[:, :main], both[:, main : 2 * main], dmixed[:, :main]))
        if main < hidden:
            gate, up = last_tile(both, 2 * main)
            rest = dmixed[:, main:]
            dgate, dup = gradients(gate, up, jnp.concatenate([rest, rest], 1))
            lane = lax.broadcasted_iota(jnp.int32, dgate.shape, 1)
            pieces.append(jnp.where(lane < HEAD_DIM, dgate, pltpu.roll(dup, HEAD_DIM, 1)))
        low = jnp.concatenate(pieces, 1).astype(jnp.bfloat16)
        if which == 0:
            grads[...] = low
        else:
            put_slot(step, low, grads_there)
        partial += contract_last(low, weight[which])
    put_slot(step, partial, outs)


def mlp_forward(slots, weights):
    length, width = slots[0].shape
    both = weights[0].shape[1]
    shape = jax.ShapeDtypeStruct
    shapes = [
        shape((4 * length, 2 * both), jnp.float32),
        shape((4 * length, both // 2), jnp.bfloat16),
    ] + [shape((length, both // 2), jnp.bfloat16)] * 4
    scratch = [
        pltpu.VMEM((length, width), jnp.bfloat16),
        pltpu.VMEM((2,) + weights[0].shape, jnp.bfloat16),
        pltpu.SemaphoreType.DMA((2, 1)),
    ]
    return run_kernel(
        hidden_kernel,
        "mlp_forward",
        4,
        [*slots, *weights],
        [fixed((length, width))] * 4 + anywhere(2),
        shapes,
        [moving((length, s.shape[1]), 0) for s in shapes[:2]] + [fixed(s.shape) for s in shapes[2:]],
        scratch,
        {},
    )


def mlp_backward(first, slots, raw, weights, carried, later=()):
    length, width = slots[0].shape
    both = weights[0][0].shape[1]
    shape = jax.ShapeDtypeStruct
    shapes = [shape((4 * length, both), jnp.bfloat16)]
    shapes += [shape((length, both), jnp.bfloat16)] * 2
    shapes += [shape((length, width), part_types(first))] * 2
    inputs = [*slots, raw, *weights[0], *weights[1], *carried]
    scratch = [
        pltpu.VMEM((length, width), jnp.bfloat16),
        pltpu.VMEM((2,) + weights[0][0].shape, jnp.bfloat16),
        pltpu.VMEM((2,) + weights[0][1].shape, jnp.bfloat16),
        pltpu.SemaphoreType.DMA((2, 2)),
    ]

    def kernel(*refs):
        hidden_back_kernel(*refs[:7], *refs[7 + len(carried) :])

    return run_kernel(
        kernel,
        "mlp_backward",
        2,
        inputs,
        [fixed((length, width))] * 2
        + [moving((length, 2 * both), first)]
        + anywhere(4 + len(carried)),
        shapes,
        [moving((length, both), first)] + [fixed(s.shape) for s in shapes[1:]],
        scratch,
        {7 + i: i for i in range(len(carried))},
        later,
    )


def mlp_output(mixed, mixed_there, weights, later=()):
    hidden, width = weights[0].shape
    length = mixed.shape[0] // 4

    def kernel(*refs):
        slots, outs, (place, weight, sems) = refs[1:5], refs[7:11], refs[11:]
        step = pl.program_id(0)
        wait = loader(step, [refs[5:6], refs[6:7]], [weight], sems)
        pick_slot(step, slots, place)
        partial = 0.0
        for which, values in enumerate((refs[0], place)):
            wait(which)
            partial += dot(values[...], weight[which])
        put_slot(step, partial, outs)

    return run_kernel(
        kernel,
        "mlp_output",
        4,
        [mixed, *mixed_there, *weights],
        [moving((length, hidden), 0)] + [fixed((length, hidden))] * 4 + anywhere(2),
        [jax.ShapeDtypeStruct((length, width), part_types(k)) for k in range(4)],
        [fixed((length, width))] * 4,
        [
            pltpu.VMEM((length, hidden), jnp.bfloat16),
            pltpu.VMEM((2, hidden, width), jnp.bfloat16),
            pltpu.SemaphoreType.DMA((2, 1)),
        ],
        {},
        later,
    )


def scalar(value):
    return value.reshape(1).astype(jnp.int32)


def place_blocks(parts, index):
    length, width = parts[0].shape

    def kernel(index_ref, *refs):
        for k, part in enumerate(refs[:-1]):
            start = pl.multiple_of((index_ref[0] ^ k) * length, length)
            refs[-1][pl.ds(start, length), :] = part[...]

    return run_kernel(
        kernel,
        "place_blocks",
        1,
        [scalar(index), *parts],
        [pl.BlockSpec(memory_space=pltpu.SMEM)] + [fixed((length, width))] * len(parts),
        jax.ShapeDtypeStruct((len(parts) * length, width), parts[0].dtype),
        fixed((len(parts) * length, width)),
        [],
        {},
    )


def split_blocks(values, index, length):
    width = values.shape[1]

    def kernel(index_ref, ref, *outs):
        for k, out in enumerate(outs):
            start = pl.multiple_of((index_ref[0] ^ k) * length, length)
            out[...] = ref[pl.ds(start, length), :]

    return run_kernel(
        kernel,
        "split_blocks",
        1,
        [scalar(index), values],
        [pl.BlockSpec(memory_space=pltpu.SMEM), fixed(values.shape)],
        [jax.ShapeDtypeStruct((length, width), values.dtype)] * 4,
        [fixed((length, width))] * 4,
        [],
        {},
    )


def pick_columns(weights, x_index, yc_index, outer, size, merge):
    rows, width = weights[0].shape
    cols = merge(*([jnp.zeros((8, outer * size), jnp.float32)] * len(weights))).shape[1]
    step, kind = min(rows, 32), weights[0].dtype

    def kernel(x_ref, yc_ref, *refs):
        sources, outs, stage = refs[: len(weights)], refs[len(weights) : -1], refs[-1]
        here = x_ref[0]
        for t in range(4):
            picked = []
            for source in sources:
                pieces = []
                for k in range(outer):
                    start = (k * 4 + t) * 2 * size
                    both = source[:, start : start + 2 * size].astype(jnp.float32)
                    pieces.append(jnp.where(here == 0, both[:, :size], both[:, size:]))
                picked.append(jnp.concatenate(pieces, 1))
            stage[t ^ yc_ref[0]] = merge(*picked).astype(kind)
        for k, out in enumerate(outs):
            out[...] = stage[k]

    return run_kernel(
        kernel,
        "pick_columns",
        rows // step,
        [scalar(x_index), scalar(yc_index), *weights],
        [pl.BlockSpec(memory_space=pltpu.SMEM)] * 2 + [moving((step, width), 0)] * len(weights),
        [jax.ShapeDtypeStruct((rows, cols), kind)] * 4,
        [moving((step, cols), 0)] * 4,
        [pltpu.VMEM((4, step, cols), kind)],
        {},
    )


def unpack_vectors(packed, shards, x_index, yc_index, outer, size):
    rows = packed.shape[1]
    width, cols = rows * shards, outer * size

    def kernel(x_ref, yc_ref, ref, out, whole, stage):
        for shard in range(shards):
            for k in range(7):
                line = jnp.broadcast_to(ref[shard * 8 + k : shard * 8 + k + 1, :], (8, rows))
                if k < 4:
                    start = k * width + shard * rows
                    out[:, start : start + rows] = line
                else:
                    start = (3 * shard + k - 4) * rows
                    whole[:, start : start + rows] = line
        for t in range(4):
            pieces = []
            for k in range(outer):
                start = (k * 4 + t) * 2 * size
                both = whole[:, start : start + 2 * size]
                pieces.append(jnp.where(x_ref[0] == 0, both[:, :size], both[:, size:]))
            stage[t ^ yc_ref[0]] = jnp.concatenate(pieces, 1)
        for k in range(2):
            start = 4 * width + k * cols
            out[:, start : start + cols] = stage[k]

    shape = (8, 4 * width + 2 * cols)
    return run_kernel(
        kernel,
        "unpack_vectors",
        1,
        [scalar(x_index), scalar(yc_index), packed],
        [pl.BlockSpec(memory_space=pltpu.SMEM)] * 2 + [fixed(packed.shape)],
        jax.ShapeDtypeStruct(shape, jnp.float32),
        fixed(shape),
        [pltpu.VMEM((8, 3 * width), jnp.float32), pltpu.VMEM((4, 8, cols), jnp.float32)],
        {},
    )


def gather_z(values):
    return lax.all_gather(values, "z", axis=0, tiled=True)


def scatter_z(values):
    return lax.psum_scatter(values, "z", scatter_dimension=0, tiled=True)


def per_device(
    tokens,
    doc_ids,
    cotangent,
    ln1_gain,
    ln1_bias,
    w_qkv,
    b_qkv,
    w_out,
    ln2_gain,
    ln2_bias,
    w_gate,
    w_up,
    w_down,
):
    x_index, z_index = lax.axis_index("x"), lax.axis_index("z")
    y_index, c_index = lax.axis_index("y"), lax.axis_index("c")
    yc_index = 2 * y_index + c_index
    planes = lax.axis_size("z")
    shards = 4 * planes
    rows = w_qkv.shape[0]
    width = rows * shards
    hidden_dim = w_gate.shape[1]
    piece = hidden_dim // (2 * shards)
    mlp = piece * planes
    head_cols = width // 8
    spread = rows % (2 * HEAD_DIM) == 0
    groups = planes if spread else 1
    unit = head_cols // groups
    length = tokens.shape[0]

    def pick_x(values, axis):
        return lax.dynamic_index_in_dim(values, x_index, axis, keepdims=False)

    def pick_yc(values, axis):
        return lax.dynamic_index_in_dim(values, yc_index, axis, keepdims=False)

    def plane_rows(blocks, later=()):
        return place_blocks(exchange(blocks, later), yc_index)

    main = mlp // 128 * 128

    def pair(gate, up):
        return jnp.concatenate([gate[:, :main], up[:, :main], gate[:, main:], up[:, main:]], 1)

    def unpair(both):
        rest = both[..., 2 * main :]
        return (
            jnp.concatenate([both[..., :main], rest[..., : mlp - main]], -1),
            jnp.concatenate([both[..., main : 2 * main], rest[..., mlp - main :]], -1),
        )

    blocks = pick_columns([w_qkv], x_index, yc_index, 3 * groups, unit, lambda v: v)
    block_qkv = plane_rows(blocks)
    lines = [v[None] for v in (ln1_gain, ln1_bias, ln2_gain, ln2_bias)]
    lines += [b_qkv.reshape(3, rows), jnp.zeros((1, rows), jnp.bfloat16)]
    packed = after(jnp.concatenate(lines, 0).astype(jnp.float32), blocks[1])
    packed = gather_direct(gather_direct(packed, ("y", "c"), 4), "z", planes)
    if spread:
        full_out = gather_z(pick_x(w_out.reshape(2, rows // 2, width), 0))
    else:
        full_out = lax.all_gather(w_out, ("z", "y", "c"), axis=0, tiled=True)
        full_out = pick_x(pick_yc(full_out.reshape(4, 2, unit, width), 0), 0)
    docs = jnp.stack(plane_gather(doc_ids))
    full_qkv = gather_z(after(block_qkv, full_out))
    token_slots = plane_gather(after(tokens, block_qkv))
    blocks = pick_columns([w_gate, w_up], x_index, yc_index, planes, piece, pair)
    block_both = plane_rows(blocks, (*token_slots[1:3], packed, docs))
    full_both = gather_z(block_both)
    full_down = gather_z(pick_x(w_down.reshape(2, piece, width), 0))

    vectors = unpack_vectors(packed, shards, x_index, yc_index, 3 * groups, unit)
    indices = jnp.arange(length, dtype=jnp.int32)
    same_doc = docs[:, :, None] == docs[:, None, :]
    first_row = jnp.min(jnp.where(same_doc, indices[None, None, :], length), axis=2)
    table = spread_rotary((indices[None] - first_row).reshape(-1))
    docs = (docs[:, :, None], docs[:, None, :])

    full_qkv = after(full_qkv, full_out, block_both, *token_slots[1:], table, *docs, vectors)
    weights = list(zip(with_sibling(full_qkv), with_sibling(full_out)))
    cot_late = after(cotangent, block_both)
    cot_near, cot_side = swap(cot_late, FIRST), swap(cot_late, SECOND)
    *carried, side_part, far_part = attention_forward(
        2, token_slots[2:], vectors, weights, docs, table, ()
    )
    normed_low, proj, lse, attended_low, own_part, near_part = attention_forward(
        0, token_slots[:2], vectors, weights, docs, table, carried, (cot_near, cot_side)
    )
    _, parts = plane_sum(own_part, near_part, side_part, far_part)
    hidden, normed_two = norm_forward(tokens, parts, vectors)

    two_slots = plane_gather(normed_two)
    both_weights = with_sibling(after(full_both, two_slots[3]))
    cot_far = swap(after(cot_near, two_slots[3]), SECOND)
    raw, mixed, *mixed_there = mlp_forward(two_slots, both_weights)
    cot_far = after(cot_far, raw)
    cot_slots = [cotangent, cot_near, cot_side, cot_far]
    def across(blocks):
        return [swap(block, SIBLING) for block in blocks]

    pairs = [(([mixed], 0), (cot_slots, 0)), ((across(mixed_there), 0), (across(cot_slots), 0))]
    down_grad = token_product(pairs, mlp, width)
    down_sum = scatter_z(down_grad)
    down_weights = with_sibling(after(full_down, down_grad))
    mlp_weights = list(zip(both_weights, down_weights))
    both_grads, *far_grads, side_part, far_part = mlp_backward(
        2, cot_slots[2:], raw, mlp_weights, (), (down_grad,)
    )
    both_grads, *near_grads, own_part, near_part = mlp_backward(
        0, cot_slots[:2], raw, mlp_weights, (both_grads,)
    )
    near_low, parts = plane_sum(own_part, near_part, side_part, far_part)
    pairs = [
        ((two_slots, 0), ([both_grads], 0)),
        ((across(two_slots), 0), (across([*near_grads, *far_grads]), 0)),
    ]
    both_grad = token_product(pairs, width, 2 * mlp, (near_low,))
    both_sum = scatter_z(both_grad)
    def whole_rows(half):
        other = swap(half, ACROSS_X)
        odd = x_index == 1
        return jnp.concatenate(
            [jnp.where(odd, other, half), jnp.where(odd, half, other)], 0
        ).astype(jnp.float32)

    grad_hidden, hidden_low, norm_sums = norm_backward(
        hidden, cotangent, parts, vectors, 1, True, (both_grad,)
    )
    near_hidden = swap(hidden_low, FIRST)
    out_parts = mlp_output(mixed, mixed_there, down_weights, (hidden_low,))

    near_hidden = after(near_hidden, out_parts[0])
    side_hidden = swap(after(hidden_low, near_hidden), SECOND)
    far_hidden = swap(near_hidden, SECOND)
    hidden_slots = [hidden_low, near_hidden, side_hidden, far_hidden]
    sums = jnp.zeros((1, 2 * width + 6 * head_cols), jnp.float32)
    common = (weights, docs, table, (proj, lse))
    grad_proj, sums, *near_proj, own_part, near_part = attention_backward(
        0, hidden_slots[:2], token_slots[:2], *common, sums, (), (out_parts[0],)
    )
    done = (own_part, *hidden_slots[2:])
    out_parts = [*out_parts[:2], *(after(part, *done) for part in out_parts[2:])]
    out_near, out_sum = plane_sum(*out_parts)
    grad_proj, sums, *far_proj, side_part, far_part = attention_backward(
        2, hidden_slots[2:], token_slots[2:], *common, sums, (grad_proj,)
    )

    placed = jnp.zeros((3 * groups, 4, 2, unit), jnp.float32)
    for k in range(2):
        piece_sum = sums[0, 2 * width + 3 * head_cols * k :][: 3 * head_cols]
        placed = lax.dynamic_update_slice(
            placed,
            piece_sum.reshape(3 * groups, 1, 1, unit),
            (0, yc_index ^ k, x_index, 0),
        )
    lines = [v[0, i * width : (i + 1) * width] for v in (sums, norm_sums) for i in range(2)]
    lines = [v.reshape(planes, 4, rows) for v in lines] + [placed.reshape(planes, 4, 3 * rows)]
    extra = jnp.concatenate(lines, 2).reshape(planes, 28 * rows)
    extra = jnp.pad(extra, ((0, 0), (0, EXTRA_ROWS * 3 * head_cols - 28 * rows)))
    extra = extra.reshape(planes * EXTRA_ROWS, 3 * head_cols).astype(jnp.bfloat16)
    pairs = [
        (([normed_low], 0), ([grad_proj], 0)),
        ((across([normed_low]), 0), (across([*near_proj, *far_proj]), 0)),
    ]
    qkv_grad = token_product(pairs, width, 3 * head_cols, (out_near,), extra)
    qkv_sum = scatter_z(qkv_grad)
    own, side, near = (part.astype(jnp.float32) for part in out_sum)
    activations = (hidden + (own + side + near)).astype(jnp.bfloat16)
    far_part, side_part = (after(part, qkv_grad) for part in (far_part, side_part))
    norm_near, parts = plane_sum(own_part, near_part, side_part, far_part)
    (d_tokens,) = norm_backward(tokens, grad_hidden, parts, vectors, 0, False)
    def whole_columns(summed):
        half = plane_rows(split_blocks(summed, yc_index, rows))
        other = swap(half, ACROSS_X)
        return [v.reshape(4, rows, summed.shape[1]) for v in (half, other)]

    owned_down = whole_rows(after(down_sum, out_near))
    gate_half, other = whole_columns(after(both_sum, owned_down))
    def out_product(window, later):
        pairs = [(([attended_low], window), (hidden_slots, 0))]
        return token_product(pairs, head_cols, width, later, us=40)

    out_there = swap(out_product(1, (gate_half, norm_near)), SIBLING)
    out_grad = out_product(0, ()).astype(jnp.float32) + out_there.astype(jnp.float32)
    out_grad = out_grad.astype(jnp.bfloat16)

    if spread:
        owned_out = whole_rows(scatter_z(out_grad))
    else:
        placed_out = lax.dynamic_update_slice(
            jnp.zeros((4, 2, unit, width), jnp.bfloat16),
            out_grad[None, None],
            (yc_index, x_index, 0, 0),
        )
        owned_out = lax.psum_scatter(
            placed_out.reshape(width, width), ("z", "y", "c"), scatter_dimension=0, tiled=True
        )
        owned_out = lax.psum(owned_out, "x").astype(jnp.float32)

    owned_gate, owned_up = spread_columns(gate_half, other, x_index, unpair, planes, piece)
    small = qkv_sum[4 * rows :].reshape(-1)[: 28 * rows].reshape(4, 7 * rows).astype(jnp.float32)
    for axis in ("c", "y", "x"):
        small = small + meet(small, axis, 1, 2)
    small = pick_yc(small, 0)
    half, other = whole_columns(after(qkv_sum, other, parts[2], out_sum[2]))
    (owned_qkv,) = spread_columns(half, other, x_index, lambda v: (v,), 3 * groups, unit)

    return (
        activations,
        d_tokens,
        small[:rows],
        small[rows : 2 * rows],
        owned_qkv,
        small[4 * rows :],
        owned_out,
        small[2 * rows : 3 * rows],
        small[3 * rows : 4 * rows],
        owned_gate,
        owned_up,
        owned_down,
    )


def solution(mesh):
    reps, shards = mesh.shape["rep"], mesh.shape["shard"]
    grid = Mesh(mesh.devices.reshape(reps, shards // 4, 2, 2), EVERY)
    tokens, rows, vector = P(EVERY, None), P(("z", "y", "c"), None), P(("z", "y", "c"))
    return jax.shard_map(
        per_device,
        mesh=grid,
        in_specs=(
            tokens,
            P(EVERY),
            tokens,
            vector,
            vector,
            rows,
            vector,
            rows,
            vector,
            vector,
            rows,
            rows,
            rows,
        ),
        out_specs=(
            tokens,
            tokens,
            vector,
            vector,
            rows,
            vector,
            rows,
            vector,
            vector,
            rows,
            rows,
            rows,
        ),
        check_vma=False,
    )
```

```python
import jax
import jax.numpy as jnp
from jax import lax
from jax.experimental import pallas as pl
from jax.experimental.pallas import tpu as pltpu
from jax.sharding import Mesh, PartitionSpec as P

HEAD_DIM = 64
ROT = 16
PLANE = ("x", "y", "c")
EVERY = ("x", "z", "y", "c")
SIBLING = (1, 1)
FIRST = (4, 2)
SECOND = (2, 4)
ACROSS_X = (4, 4)
ACROSS_Y = (2, 2)
ACROSS_YC = (3, 3)
VMEM_BYTES = 48 << 20
EXTRA_ROWS = 16
MICROSECONDS = {
    "attention_forward": 15,
    "attention_backward": 27,
    "mlp_forward": 8,
    "mlp_backward": 21,
    "mlp_output": 18,
    "token_product": 14,
    "norm_forward": 5,
    "norm_backward": 5,
    "spread_columns": 4,
    "pick_columns": 3,
    "place_blocks": 1,
    "split_blocks": 1,
    "unpack_vectors": 1,
    "after": 0,
}


def cost(name):
    return cost_of(MICROSECONDS[name])


def cost_of(us):
    flops = us * 1_150_000_000 + 1_000_000
    return pl.CostEstimate(flops=flops, bytes_accessed=1 << 10, transcendentals=0)


def swap(values, masks):
    pairs = [(i, i ^ masks[i & 1]) for i in range(8)]
    return lax.ppermute(values, PLANE, pairs)


def plane_gather(values):
    side = swap(values, SECOND)
    near = after(swap(values, FIRST), side)
    return [values, near, side, swap(near, SECOND)]


def plane_sum(own, near, side, far, later=()):
    far = swap(far, SECOND)
    side = swap(side, SECOND)
    near = after((near + far.astype(jnp.float32)).astype(jnp.bfloat16), side, *later)

    return near, (own, side, swap(near, FIRST))


def with_sibling(values):
    return [values, swap(values, SIBLING)]


def exchange(blocks, later=()):
    if later:
        blocks = [blocks[0]] + [after(block, *later) for block in blocks[1:]]
    blocks, masks = list(blocks), (None, SIBLING, ACROSS_Y, ACROSS_YC)
    return blocks[:1] + [swap(blocks[k], masks[k]) for k in range(1, 4)]


def meet(values, axis, bit, size):
    return lax.ppermute(values, axis, [(i, i ^ bit) for i in range(size)])


def gather_direct(block, axis, size):
    parts = [block] + [meet(block, axis, k, size) for k in range(1, size)]
    return place_blocks(parts, lax.axis_index(axis))


def layer_norm(values, gain_vec, bias_vec):
    average = jnp.mean(values, -1, keepdims=True)
    centered = values - average
    recip_std = lax.rsqrt(jnp.mean(centered * centered, -1, keepdims=True) + 1e-05)
    unit_vals = centered * recip_std
    return (unit_vals * gain_vec + bias_vec, unit_vals, recip_std)


def norm_back(grad_in, unit_vals, recip_std, gain_vec):
    scaled = grad_in * gain_vec
    return recip_std * (
        scaled
        - jnp.mean(scaled, -1, keepdims=True)
        - unit_vals * jnp.mean(scaled * unit_vals, -1, keepdims=True)
    )


def dot(left, right):
    return jnp.dot(left, right, preferred_element_type=jnp.float32)


def contract_last(left, right):
    return lax.dot_general(
        left, right, (((1,), (1,)), ((), ())), preferred_element_type=jnp.float32
    )


def contract_first(left, right):
    return lax.dot_general(
        left, right, (((0,), (0,)), ((), ())), preferred_element_type=jnp.float32
    )


def spread_rotary(positions):
    half_rot = ROT // 2
    frequency = 10000.0 ** (-(jnp.arange(half_rot, dtype=jnp.float32) * 2.0 / ROT))
    lane = jnp.arange(2 * HEAD_DIM) % HEAD_DIM
    frequency = jnp.where(lane < ROT, jnp.tile(frequency, 2 * HEAD_DIM // half_rot), 0.0)
    angles = positions.astype(jnp.float32)[:, None] * frequency
    sine = jnp.sin(angles)
    from_right = jnp.where(lane < half_rot, -sine, 0.0)
    from_left = jnp.where(lane < half_rot, 0.0, sine)
    return jnp.concatenate([jnp.cos(angles), from_right, from_left], 1)


def turn(values, table, direction):
    cols, lanes = values.shape[1], 2 * HEAD_DIM
    times = cols // lanes
    wide = [jnp.concatenate([table[:, k * lanes : (k + 1) * lanes]] * times, 1) for k in range(3)]
    half_rot = ROT // 2
    from_right = pltpu.roll(values, cols - half_rot, 1) * wide[1]
    from_left = pltpu.roll(values, half_rot, 1) * wide[2]
    return values * wide[0] + direction * (from_right + from_left)


def head_mask(head, shape):
    lane = lax.broadcasted_iota(jnp.int32, shape, 1)
    return (lane >= head * HEAD_DIM) & (lane < (head + 1) * HEAD_DIM)


def visible(docs_col, docs_row):
    shape = (docs_col.shape[0], docs_row.shape[1])
    row = lax.broadcasted_iota(jnp.int32, shape, 0)
    col = lax.broadcasted_iota(jnp.int32, shape, 1)
    return (docs_col == docs_row) & (col <= row)


def by_head(values):
    heads = values.shape[1] // HEAD_DIM
    zero = jnp.zeros_like(values)
    return jnp.concatenate(
        [jnp.where(head_mask(head, values.shape), values, zero) for head in range(heads)], 0
    )


def join_heads(stacked):
    heads = stacked.shape[1] // HEAD_DIM
    rows = stacked.shape[0] // heads
    joined = stacked[:rows]
    for head in range(1, heads):
        part = stacked[head * rows : (head + 1) * rows]
        joined = jnp.where(head_mask(head, part.shape), part, joined)
    return joined


def head_scores(query_heads, key, allowed):
    return jnp.where(allowed, contract_last(query_heads, key) * 0.125, -1e30)


def pick_slot(step, slots, place):
    for k, slot in enumerate(slots):

        @pl.when(step == k)
        def _(slot=slot):
            place[...] = slot[...]


def put_slot(step, value, slots):
    for k, slot in enumerate(slots):

        @pl.when(step == k)
        def _(slot=slot):
            slot[...] = value.astype(slot.dtype)


def loader(step, sources, places, sems, order=(0,)):
    def fetch(which, k):
        return pltpu.make_async_copy(sources[which][k], places[k].at[which], sems.at[which, k])

    @pl.when(step == 0)
    def _():
        for which in range(2):
            for k in order:
                fetch(which, k).start()

    def wait(which, k=0):
        @pl.when(step == 0)
        def _():
            fetch(which, k).wait()

    return wait


def forward_kernel(first, *refs):
    slots, refs = refs[:2], refs[2:]
    vectors, docs_col, docs_row, table = refs[:4]
    weights = [refs[4:6], refs[6:8]]
    outs, (place, weight, weight_out, sems) = refs[-10:-4], refs[-4:]
    normed, proj, lse, attended = outs[:4]
    step = pl.program_id(0)
    wait = loader(step, weights, [weight, weight_out], sems, (0, 1))
    pick_slot(step, slots, place)
    width = normed.shape[1]
    gain, bias = vectors[:1, :width], vectors[:1, width : 2 * width]
    values, _, _ = layer_norm(place[...].astype(jnp.float32), gain, bias)
    low = values.astype(jnp.bfloat16)
    normed[...] = low
    allowed = visible(docs_col[0], docs_row[0])
    allowed = jnp.concatenate([allowed] * (weight_out.shape[1] // HEAD_DIM), 0)
    lane = lax.broadcasted_iota(jnp.int32, lse.shape, 1)
    logs = jnp.zeros(lse.shape, jnp.float32)
    partial = 0.0
    cols = weight_out.shape[1]
    heads = cols // HEAD_DIM
    for which in range(2):
        wait(which)
        start = 4 * width + 3 * cols * which
        whole = dot(low, weight[which]) + vectors[:1, start : start + 3 * cols]
        turned = turn(whole[:, : 2 * cols], table[...], 1.0)
        turned = turned.astype(jnp.bfloat16)
        query, key = turned[:, :cols], turned[:, cols:]
        value = whole[:, 2 * cols :].astype(jnp.bfloat16)
        start = 3 * cols * which
        proj[:, start : start + 2 * cols] = turned
        proj[:, start + 2 * cols : start + 3 * cols] = value
        scores = head_scores(by_head(query), key, allowed)
        highest = jnp.max(scores, -1, keepdims=True)
        powers = jnp.exp(scores - highest)
        total = jnp.sum(powers, -1, keepdims=True)
        probs = (powers * (1.0 / total)).astype(jnp.bfloat16)
        joined = join_heads(dot(probs, value))
        log_total = highest + jnp.log(total)
        rows = query.shape[0]
        for head in range(heads):
            part = log_total[head * rows : (head + 1) * rows]
            logs = jnp.where(lane == heads * which + head, part, logs)
        low_joined = joined.astype(jnp.bfloat16)
        attended[:, cols * which : cols * (which + 1)] = low_joined
        wait(which, 1)
        partial += dot(low_joined, weight_out[which])
    lse[...] = logs
    put_slot(step, partial, outs[4:])


def backward_kernel(count, *refs):
    slots, tokens, refs = refs[:count], refs[count : 2 * count], refs[2 * count :]
    docs_col, docs_row, table, proj, lse, sums_in = refs[:6]
    weights = [refs[6:8], refs[8:10]]
    outs, (place, inputs, weight, weight_out, sems) = refs[-7 - 2 * count : -5], refs[-5:]
    dproj, sums, dproj_there = outs[0], outs[1], outs[2 : 2 + count]
    step = pl.program_id(0)
    wait = loader(step, weights, [weight, weight_out], sems, (1, 0))
    pick_slot(step, slots, place)
    pick_slot(step, tokens, inputs)

    @pl.when(step == 0)
    def _():
        sums[...] = sums_in[...]

    grad = place[...]
    cols = weight_out.shape[1]
    heads = cols // HEAD_DIM
    allowed = visible(docs_col[0], docs_row[0])
    allowed = jnp.concatenate([allowed] * heads, 0)
    width = grad.shape[1]
    dnorm = 0.0
    for which in range(2):
        wait(which, 1)
        datt = contract_last(grad, weight_out[which]).astype(jnp.bfloat16)
        start = 3 * cols * which
        query, key, value = (
            proj[:, start + i * cols : start + (i + 1) * cols] for i in range(3)
        )
        query_heads, datt_heads = by_head(query), by_head(datt)
        scores = head_scores(query_heads, key, allowed)
        log_total = jnp.concatenate(
            [lse[:, heads * which + head : heads * which + head + 1] for head in range(heads)], 0
        )
        probs = jnp.exp(scores - log_total)
        dvalue = contract_first(probs.astype(jnp.bfloat16), datt_heads)
        dprobs = contract_last(datt_heads, value)
        inner = jnp.sum(probs * dprobs, -1, keepdims=True)
        dscores = (0.125 * probs * (dprobs - inner)).astype(jnp.bfloat16)
        dquery = join_heads(dot(dscores, key))
        dkey = contract_first(dscores, query_heads)
        turned = turn(jnp.concatenate([dquery, dkey], 1), table[...], -1.0)
        low = jnp.concatenate([turned, dvalue], 1).astype(jnp.bfloat16)
        if which == 0:
            dproj[...] = low
        else:
            put_slot(step, low, dproj_there)
        wait(which)
        dnorm += contract_last(low, weight[which])
        start += 2 * width
        sums[:, start : start + 3 * cols] += jnp.sum(low.astype(jnp.float32), 0, keepdims=True)
    put_slot(step, dnorm, outs[2 + count :])
    values = inputs[...].astype(jnp.float32)
    centered = values - jnp.mean(values, -1, keepdims=True)
    unit = centered * lax.rsqrt(jnp.mean(centered * centered, -1, keepdims=True) + 1e-05)
    sums[:, :width] += jnp.sum(dnorm * unit, 0, keepdims=True)
    sums[:, width : 2 * width] += jnp.sum(dnorm, 0, keepdims=True)


def standardized(values):
    centered = values - jnp.mean(values, -1, keepdims=True)
    recip_std = lax.rsqrt(jnp.mean(centered * centered, -1, keepdims=True) + 1e-05)
    return centered * recip_std, recip_std


def norm_forward(tokens, parts, vectors):
    length, width = tokens.shape
    step = length // 4

    def kernel(token_ref, own, side, near, vec, hidden, low):
        total = own[...] + side[...].astype(jnp.float32) + near[...].astype(jnp.float32)
        total += token_ref[...].astype(jnp.float32)
        hidden[...] = total
        unit, _ = standardized(total)
        gain, bias = vec[:1, 2 * width : 3 * width], vec[:1, 3 * width : 4 * width]
        low[...] = (unit * gain + bias).astype(jnp.bfloat16)

    block = moving((step, width), 0)
    return run_kernel(
        kernel,
        "norm_forward",
        4,
        [tokens, *parts, vectors],
        [block] * 4 + [fixed(vectors.shape)],
        [jax.ShapeDtypeStruct((length, width), d) for d in (jnp.float32, jnp.bfloat16)],
        [block] * 2,
        [],
        {},
    )


def norm_backward(values, straight, parts, vectors, which, with_sums, later=()):
    length, width = values.shape
    step = length // 4

    def kernel(value_ref, straight_ref, own, side, near, vec, total, *more):
        grad = own[...] + side[...].astype(jnp.float32) + near[...].astype(jnp.float32)
        unit, recip_std = standardized(value_ref[...].astype(jnp.float32))
        gain = vec[:1, 2 * which * width : (2 * which + 1) * width]
        back = norm_back(grad, unit, recip_std, gain)
        back += straight_ref[...].astype(jnp.float32)
        total[...] = back
        if with_sums:
            low, sums = more
            low[...] = back.astype(jnp.bfloat16)

            @pl.when(pl.program_id(0) == 0)
            def _():
                sums[...] = jnp.zeros_like(sums)

            sums[:, :width] += jnp.sum(grad * unit, 0, keepdims=True)
            sums[:, width:] += jnp.sum(grad, 0, keepdims=True)

    block = moving((step, width), 0)
    shape = jax.ShapeDtypeStruct
    shapes, specs = [shape((length, width), jnp.float32)], [block]
    if with_sums:
        shapes += [shape((length, width), jnp.bfloat16), shape((1, 2 * width), jnp.float32)]
        specs += [block, fixed((1, 2 * width))]
    return run_kernel(
        kernel,
        "norm_backward",
        4,
        [values, straight, *parts, vectors],
        [block] * 5 + [fixed(vectors.shape)],
        shapes,
        specs,
        [],
        {},
        later,
    )


def fixed(shape):
    return pl.BlockSpec(shape, lambda i: (0,) * len(shape))


def moving(shape, first):
    return pl.BlockSpec(shape, lambda i: (first + i,) + (0,) * (len(shape) - 1))


def anywhere(count):
    return [pl.BlockSpec(memory_space=pl.ANY)] * count


def run_kernel(
    kernel, name, blocks, inputs, in_specs, shapes, out_specs, scratch, aliases, later=(), us=None
):
    given, used = len(later), kernel
    if given:

        def used(*refs):
            kernel(*refs[given:])

    aliases = {k + given: v for k, v in aliases.items()}
    return pl.pallas_call(
        used,
        grid=(blocks,),
        out_shape=shapes,
        in_specs=anywhere(given) + in_specs,
        out_specs=out_specs,
        scratch_shapes=scratch,
        input_output_aliases=aliases,
        compiler_params=pltpu.CompilerParams(vmem_limit_bytes=VMEM_BYTES),
        cost_estimate=cost(name) if us is None else cost_of(us),
        name=name,
    )(*later, *inputs)


def after(value, *others, us=0):
    return pl.pallas_call(
        lambda *refs: None,
        out_shape=jax.ShapeDtypeStruct(value.shape, value.dtype),
        in_specs=anywhere(1 + len(others)),
        out_specs=pl.BlockSpec(memory_space=pl.ANY),
        input_output_aliases={0: 0},
        cost_estimate=cost_of(us),
        name="after",
    )(value, *others)


def part_types(first):
    return jnp.bfloat16 if first >= 2 else jnp.float32


def attention_forward(first, slots, vectors, weights, docs, table, carried, later=()):
    length, width = slots[0].shape
    cols = weights[0][1].shape[0]
    shape = jax.ShapeDtypeStruct
    shapes = [
        shape((4 * length, width), jnp.bfloat16),
        shape((4 * length, 6 * cols), jnp.bfloat16),
        shape((4 * length, 128), jnp.float32),
        shape((4 * length, 2 * cols), jnp.bfloat16),
    ] + [shape((length, width), part_types(first))] * 2
    inputs = [*slots, vectors, *docs, table, *weights[0], *weights[1], *carried]
    in_specs = (
        [fixed((length, width))] * 2
        + [fixed(vectors.shape)]
        + [moving((1, length, 1), first), moving((1, 1, length), first)]
        + [moving((length, table.shape[1]), first)]
        + anywhere(4 + len(carried))
    )
    out_specs = [moving((length, s.shape[1]), first) for s in shapes[:4]]
    out_specs += [fixed((length, width))] * 2
    scratch = [
        pltpu.VMEM((length, width), jnp.bfloat16),
        pltpu.VMEM((2,) + weights[0][0].shape, jnp.bfloat16),
        pltpu.VMEM((2,) + weights[0][1].shape, jnp.bfloat16),
        pltpu.SemaphoreType.DMA((2, 2)),
    ]
    aliases = {len(inputs) - len(carried) + i: i for i in range(len(carried))}

    def kernel(*refs):
        forward_kernel(first, *refs)

    return run_kernel(
        kernel,
        "attention_forward",
        2,
        inputs,
        in_specs,
        shapes,
        out_specs,
        scratch,
        aliases,
        later,
    )


def attention_backward(
    first, slots, tokens, weights, docs, table, kept, sums, carried, later=()
):
    length, width = slots[0].shape
    cols, count = weights[0][1].shape[0], len(slots)
    shape = jax.ShapeDtypeStruct
    shapes = [shape((4 * length, 3 * cols), jnp.bfloat16), shape(sums.shape, jnp.float32)]
    shapes += [shape((length, 3 * cols), jnp.bfloat16)] * count
    shapes += [shape((length, width), part_types(first))] * count
    inputs = [*slots, *tokens, *docs, table, *kept, sums, *weights[0], *weights[1], *carried]
    in_specs = (
        [fixed((length, width))] * (2 * count)
        + [moving((1, length, 1), first), moving((1, 1, length), first)]
        + [moving((length, table.shape[1]), first)]
        + [moving((length, k.shape[1]), first) for k in kept]
        + [fixed(sums.shape)]
        + anywhere(4 + len(carried))
    )
    out_specs = [moving((length, 3 * cols), first)] + [fixed(s.shape) for s in shapes[1:]]
    scratch = [pltpu.VMEM((length, width), jnp.bfloat16)] * 2 + [
        pltpu.VMEM((2,) + weights[0][0].shape, jnp.bfloat16),
        pltpu.VMEM((2,) + weights[0][1].shape, jnp.bfloat16),
        pltpu.SemaphoreType.DMA((2, 2)),
    ]

    def kernel(*refs):
        backward_kernel(count, *refs)

    return run_kernel(
        kernel,
        "attention_backward",
        count,
        inputs,
        in_specs,
        shapes,
        out_specs,
        scratch,
        {len(inputs) - len(carried): 0} if carried else {},
        later,
    )


def token_product(pairs, rows, cols, later=(), extra=None, us=None):
    by_rows, step = rows % 512 == 0, 512
    if extra is not None:
        step = rows * EXTRA_ROWS // extra.shape[0]
    grid = (rows if by_rows else cols) // step

    def fixed_columns(length, size, window):
        return pl.BlockSpec((length, size), lambda i: (0, window))

    def step_columns(length, window):
        return pl.BlockSpec((length, step), lambda i: (0, window * grid + i))

    sides, inputs, specs = [[], []], [], []
    for pair in pairs:
        for side, (blocks, window) in enumerate(pair):
            for block in blocks:
                sides[side].append((len(inputs), block.shape[0]))
                inputs.append(block)
                if by_rows == (side == 0):
                    specs.append(step_columns(block.shape[0], window))
                else:
                    specs.append(fixed_columns(block.shape[0], (rows, cols)[side], window))
    tokens = sum(length for _, length in sides[0])
    shape, place = (rows, cols), pl.BlockSpec((step, cols), lambda i: (i, 0))
    if not by_rows:
        place = pl.BlockSpec((rows, step), lambda i: (0, i))
    if extra is not None:
        inputs, specs = inputs + [extra], specs + [moving((EXTRA_ROWS, cols), 0)]
        place = moving((step + EXTRA_ROWS, cols), 0)
        shape = (rows + extra.shape[0], cols)

    def kernel(*refs):
        out, left, right = refs[-3:]

        def fill(side, whole):
            start = 0
            for k, length in sides[side]:
                whole[start : start + length, :] = refs[k][...]
                start += length

        moved, kept = (0, 1) if by_rows else (1, 0)
        wholes = (left, right)
        fill(moved, wholes[moved])

        @pl.when(pl.program_id(0) == 0)
        def _():
            fill(kept, wholes[kept])

        total = contract_first(left[...], right[...]).astype(out.dtype)
        if extra is None:
            out[...] = total
        else:
            out[:step, :] = total
            out[step:, :] = refs[-4][...]

    left_cols, right_cols = (step, cols) if by_rows else (rows, step)
    return run_kernel(
        kernel,
        "token_product",
        grid,
        inputs,
        specs,
        jax.ShapeDtypeStruct(shape, jnp.bfloat16),
        place,
        [pltpu.VMEM((tokens, size), jnp.bfloat16) for size in (left_cols, right_cols)],
        {},
        later,
        us,
    )


def spread_columns(half, other, x_index, split, outer, size):
    blocks, rows, cols = half.shape
    width = 8 * outer * size
    outs = len(split(jnp.zeros((8, cols), jnp.float32)))
    step = min(rows, 32)

    def kernel(x_ref, half_ref, other_ref, *out_refs):
        here = x_ref[0]
        for t in range(blocks):
            mine, theirs = half_ref[t].astype(jnp.float32), other_ref[t].astype(jnp.float32)
            for x in range(2):
                columns = split(jnp.where(here == x, mine, theirs))
                for out, values in zip(out_refs, columns):
                    for k in range(outer):
                        start = ((k * blocks + t) * 2 + x) * size
                        out[:, start : start + size] = values[:, k * size : (k + 1) * size]

    block = pl.BlockSpec((blocks, step, cols), lambda i: (0, i, 0))
    return run_kernel(
        kernel,
        "spread_columns",
        rows // step,
        [scalar(x_index), half, other],
        [pl.BlockSpec(memory_space=pltpu.SMEM), block, block],
        [jax.ShapeDtypeStruct((rows, width), jnp.float32)] * outs,
        [pl.BlockSpec((step, width), lambda i: (i, 0))] * outs,
        [],
        {},
    )


def last_tile(values, start):
    tile = values[:, start:]
    return tile, pltpu.roll(tile, HEAD_DIM, 1)


def hidden_kernel(*refs):
    slots, weights, refs = refs[:4], refs[4:6], refs[6:]
    raw, mixed, mixed_there, (place, weight, sems) = refs[0], refs[1], refs[2:6], refs[6:]
    step = pl.program_id(0)
    wait = loader(step, [weights[:1], weights[1:]], [weight], sems)
    pick_slot(step, slots, place)
    cols, hidden = weight.shape[2], mixed.shape[1]
    main = hidden // 128 * 128

    def mix(gate, up):
        return (gate * jax.nn.sigmoid(gate) * up).astype(jnp.bfloat16)

    for which in range(2):
        wait(which)
        both = dot(place[...], weight[which])
        raw[:, which * cols : (which + 1) * cols] = both
        pieces = [mix(both[:, :main], both[:, main : 2 * main])]
        if main < hidden:
            pieces.append(mix(*last_tile(both, 2 * main))[:, : hidden - main])
        low = jnp.concatenate(pieces, 1)
        if which == 0:
            mixed[...] = low
        else:
            put_slot(step, low, mixed_there)


def hidden_back_kernel(*refs):
    slots, raw, refs = refs[:2], refs[2], refs[3:]
    weights = [refs[0:2], refs[2:4]]
    grads, grads_there, outs = refs[-9], refs[-8:-6], refs[-6:-4]
    grad_out, weight, weight_down, sems = refs[-4:]
    step = pl.program_id(0)
    wait = loader(step, weights, [weight, weight_down], sems, (1, 0))
    pick_slot(step, slots, grad_out)
    cols, hidden = weight.shape[2], weight_down.shape[1]
    main = hidden // 128 * 128

    def gradients(gate, up, dm):
        sig = jax.nn.sigmoid(gate)
        return dm * up * sig * (1.0 + gate * (1.0 - sig)), dm * gate * sig

    partial = 0.0
    for which in range(2):
        wait(which, 1)
        dmixed = contract_last(grad_out[...], weight_down[which])
        both = raw[:, which * cols : (which + 1) * cols]
        pieces = list(gradients(both[:, :main], both[:, main : 2 * main], dmixed[:, :main]))
        if main < hidden:
            gate, up = last_tile(both, 2 * main)
            rest = dmixed[:, main:]
            dgate, dup = gradients(gate, up, jnp.concatenate([rest, rest], 1))
            lane = lax.broadcasted_iota(jnp.int32, dgate.shape, 1)
            pieces.append(jnp.where(lane < HEAD_DIM, dgate, pltpu.roll(dup, HEAD_DIM, 1)))
        low = jnp.concatenate(pieces, 1).astype(jnp.bfloat16)
        if which == 0:
            grads[...] = low
        else:
            put_slot(step, low, grads_there)
        wait(which)
        partial += contract_last(low, weight[which])
    put_slot(step, partial, outs)


def mlp_forward(slots, weights):
    length, width = slots[0].shape
    both = weights[0].shape[1]
    shape = jax.ShapeDtypeStruct
    shapes = [
        shape((4 * length, 2 * both), jnp.float32),
        shape((4 * length, both // 2), jnp.bfloat16),
    ] + [shape((length, both // 2), jnp.bfloat16)] * 4
    scratch = [
        pltpu.VMEM((length, width), jnp.bfloat16),
        pltpu.VMEM((2,) + weights[0].shape, jnp.bfloat16),
        pltpu.SemaphoreType.DMA((2, 1)),
    ]
    return run_kernel(
        hidden_kernel,
        "mlp_forward",
        4,
        [*slots, *weights],
        [fixed((length, width))] * 4 + anywhere(2),
        shapes,
        [moving((length, s.shape[1]), 0) for s in shapes[:2]] + [fixed(s.shape) for s in shapes[2:]],
        scratch,
        {},
    )


def mlp_backward(first, slots, raw, weights, carried, later=()):
    length, width = slots[0].shape
    both = weights[0][0].shape[1]
    shape = jax.ShapeDtypeStruct
    shapes = [shape((4 * length, both), jnp.bfloat16)]
    shapes += [shape((length, both), jnp.bfloat16)] * 2
    shapes += [shape((length, width), part_types(first))] * 2
    inputs = [*slots, raw, *weights[0], *weights[1], *carried]
    scratch = [
        pltpu.VMEM((length, width), jnp.bfloat16),
        pltpu.VMEM((2,) + weights[0][0].shape, jnp.bfloat16),
        pltpu.VMEM((2,) + weights[0][1].shape, jnp.bfloat16),
        pltpu.SemaphoreType.DMA((2, 2)),
    ]

    def kernel(*refs):
        hidden_back_kernel(*refs[:7], *refs[7 + len(carried) :])

    return run_kernel(
        kernel,
        "mlp_backward",
        2,
        inputs,
        [fixed((length, width))] * 2
        + [moving((length, 2 * both), first)]
        + anywhere(4 + len(carried)),
        shapes,
        [moving((length, both), first)] + [fixed(s.shape) for s in shapes[1:]],
        scratch,
        {7 + i: i for i in range(len(carried))},
        later,
    )


def mlp_output(mixed, mixed_there, weights, later=()):
    hidden, width = weights[0].shape
    length = mixed.shape[0] // 4

    def kernel(*refs):
        slots, outs, (place, weight, sems) = refs[1:5], refs[7:11], refs[11:]
        step = pl.program_id(0)
        wait = loader(step, [refs[5:6], refs[6:7]], [weight], sems)
        pick_slot(step, slots, place)
        partial = 0.0
        for which, values in enumerate((refs[0], place)):
            wait(which)
            partial += dot(values[...], weight[which])
        put_slot(step, partial, outs)

    return run_kernel(
        kernel,
        "mlp_output",
        4,
        [mixed, *mixed_there, *weights],
        [moving((length, hidden), 0)] + [fixed((length, hidden))] * 4 + anywhere(2),
        [jax.ShapeDtypeStruct((length, width), part_types(k)) for k in range(4)],
        [fixed((length, width))] * 4,
        [
            pltpu.VMEM((length, hidden), jnp.bfloat16),
            pltpu.VMEM((2, hidden, width), jnp.bfloat16),
            pltpu.SemaphoreType.DMA((2, 1)),
        ],
        {},
        later,
    )


def scalar(value):
    return value.reshape(1).astype(jnp.int32)


def place_blocks(parts, index):
    length, width = parts[0].shape

    def kernel(index_ref, *refs):
        for k, part in enumerate(refs[:-1]):
            start = pl.multiple_of((index_ref[0] ^ k) * length, length)
            refs[-1][pl.ds(start, length), :] = part[...]

    return run_kernel(
        kernel,
        "place_blocks",
        1,
        [scalar(index), *parts],
        [pl.BlockSpec(memory_space=pltpu.SMEM)] + [fixed((length, width))] * len(parts),
        jax.ShapeDtypeStruct((len(parts) * length, width), parts[0].dtype),
        fixed((len(parts) * length, width)),
        [],
        {},
    )


def split_blocks(values, index, length):
    width = values.shape[1]

    def kernel(index_ref, ref, *outs):
        for k, out in enumerate(outs):
            start = pl.multiple_of((index_ref[0] ^ k) * length, length)
            out[...] = ref[pl.ds(start, length), :]

    return run_kernel(
        kernel,
        "split_blocks",
        1,
        [scalar(index), values],
        [pl.BlockSpec(memory_space=pltpu.SMEM), fixed(values.shape)],
        [jax.ShapeDtypeStruct((length, width), values.dtype)] * 4,
        [fixed((length, width))] * 4,
        [],
        {},
    )


def pick_columns(weights, x_index, yc_index, outer, size, merge):
    rows, width = weights[0].shape
    cols = merge(*([jnp.zeros((8, outer * size), jnp.float32)] * len(weights))).shape[1]
    step, kind = min(rows, 32), weights[0].dtype

    def kernel(x_ref, yc_ref, *refs):
        sources, outs, stage = refs[: len(weights)], refs[len(weights) : -1], refs[-1]
        here = x_ref[0]
        for t in range(4):
            picked = []
            for source in sources:
                pieces = []
                for k in range(outer):
                    start = (k * 4 + t) * 2 * size
                    both = source[:, start : start + 2 * size].astype(jnp.float32)
                    pieces.append(jnp.where(here == 0, both[:, :size], both[:, size:]))
                picked.append(jnp.concatenate(pieces, 1))
            stage[t ^ yc_ref[0]] = merge(*picked).astype(kind)
        for k, out in enumerate(outs):
            out[...] = stage[k]

    return run_kernel(
        kernel,
        "pick_columns",
        rows // step,
        [scalar(x_index), scalar(yc_index), *weights],
        [pl.BlockSpec(memory_space=pltpu.SMEM)] * 2 + [moving((step, width), 0)] * len(weights),
        [jax.ShapeDtypeStruct((rows, cols), kind)] * 4,
        [moving((step, cols), 0)] * 4,
        [pltpu.VMEM((4, step, cols), kind)],
        {},
    )


def unpack_vectors(packed, shards, x_index, yc_index, outer, size):
    rows = packed.shape[1]
    width, cols = rows * shards, outer * size

    def kernel(x_ref, yc_ref, ref, out, whole, stage):
        for shard in range(shards):
            for k in range(7):
                line = jnp.broadcast_to(ref[shard * 8 + k : shard * 8 + k + 1, :], (8, rows))
                if k < 4:
                    start = k * width + shard * rows
                    out[:, start : start + rows] = line
                else:
                    start = (3 * shard + k - 4) * rows
                    whole[:, start : start + rows] = line
        for t in range(4):
            pieces = []
            for k in range(outer):
                start = (k * 4 + t) * 2 * size
                both = whole[:, start : start + 2 * size]
                pieces.append(jnp.where(x_ref[0] == 0, both[:, :size], both[:, size:]))
            stage[t ^ yc_ref[0]] = jnp.concatenate(pieces, 1)
        for k in range(2):
            start = 4 * width + k * cols
            out[:, start : start + cols] = stage[k]

    shape = (8, 4 * width + 2 * cols)
    return run_kernel(
        kernel,
        "unpack_vectors",
        1,
        [scalar(x_index), scalar(yc_index), packed],
        [pl.BlockSpec(memory_space=pltpu.SMEM)] * 2 + [fixed(packed.shape)],
        jax.ShapeDtypeStruct(shape, jnp.float32),
        fixed(shape),
        [pltpu.VMEM((8, 3 * width), jnp.float32), pltpu.VMEM((4, 8, cols), jnp.float32)],
        {},
    )


def gather_z(values):
    return lax.all_gather(values, "z", axis=0, tiled=True)


def scatter_z(values):
    return lax.psum_scatter(values, "z", scatter_dimension=0, tiled=True)


def per_device(
    tokens,
    doc_ids,
    cotangent,
    ln1_gain,
    ln1_bias,
    w_qkv,
    b_qkv,
    w_out,
    ln2_gain,
    ln2_bias,
    w_gate,
    w_up,
    w_down,
):
    x_index, z_index = lax.axis_index("x"), lax.axis_index("z")
    y_index, c_index = lax.axis_index("y"), lax.axis_index("c")
    yc_index = 2 * y_index + c_index
    planes = lax.axis_size("z")
    shards = 4 * planes
    rows = w_qkv.shape[0]
    width = rows * shards
    hidden_dim = w_gate.shape[1]
    piece = hidden_dim // (2 * shards)
    mlp = piece * planes
    head_cols = width // 8
    spread = rows % (2 * HEAD_DIM) == 0
    groups = planes if spread else 1
    unit = head_cols // groups
    length = tokens.shape[0]

    def pick_x(values, axis):
        return lax.dynamic_index_in_dim(values, x_index, axis, keepdims=False)

    def pick_yc(values, axis):
        return lax.dynamic_index_in_dim(values, yc_index, axis, keepdims=False)

    def plane_rows(blocks, later=()):
        return place_blocks(exchange(blocks, later), yc_index)

    main = mlp // 128 * 128

    def pair(gate, up):
        return jnp.concatenate([gate[:, :main], up[:, :main], gate[:, main:], up[:, main:]], 1)

    def unpair(both):
        rest = both[..., 2 * main :]
        return (
            jnp.concatenate([both[..., :main], rest[..., : mlp - main]], -1),
            jnp.concatenate([both[..., main : 2 * main], rest[..., mlp - main :]], -1),
        )

    blocks = pick_columns([w_qkv], x_index, yc_index, 3 * groups, unit, lambda v: v)
    block_qkv = plane_rows(blocks)
    lines = [v[None] for v in (ln1_gain, ln1_bias, ln2_gain, ln2_bias)]
    lines += [b_qkv.reshape(3, rows), jnp.zeros((1, rows), jnp.bfloat16)]
    packed = after(jnp.concatenate(lines, 0).astype(jnp.float32), blocks[1])
    packed = gather_direct(gather_direct(packed, ("y", "c"), 4), "z", planes)
    if spread:
        full_out = gather_z(pick_x(w_out.reshape(2, rows // 2, width), 0))
    else:
        full_out = lax.all_gather(w_out, ("z", "y", "c"), axis=0, tiled=True)
        full_out = pick_x(pick_yc(full_out.reshape(4, 2, unit, width), 0), 0)
    docs = jnp.stack(plane_gather(doc_ids))
    full_qkv = gather_z(after(block_qkv, full_out))
    token_slots = plane_gather(after(tokens, block_qkv))
    blocks = pick_columns([w_gate, w_up], x_index, yc_index, planes, piece, pair)
    block_both = plane_rows(blocks, (*token_slots[1:3], packed, docs))
    full_both = gather_z(block_both)
    full_down = gather_z(pick_x(w_down.reshape(2, piece, width), 0))

    vectors = unpack_vectors(packed, shards, x_index, yc_index, 3 * groups, unit)
    indices = jnp.arange(length, dtype=jnp.int32)
    same_doc = docs[:, :, None] == docs[:, None, :]
    first_row = jnp.min(jnp.where(same_doc, indices[None, None, :], length), axis=2)
    table = spread_rotary((indices[None] - first_row).reshape(-1))
    docs = (docs[:, :, None], docs[:, None, :])

    full_qkv = after(full_qkv, full_out, block_both, *token_slots[1:], table, *docs, vectors)
    weights = list(zip(with_sibling(full_qkv), with_sibling(full_out)))
    cot_late = after(cotangent, block_both)
    cot_near, cot_side = swap(cot_late, FIRST), swap(cot_late, SECOND)
    *carried, side_part, far_part = attention_forward(
        2, token_slots[2:], vectors, weights, docs, table, ()
    )
    normed_low, proj, lse, attended_low, own_part, near_part = attention_forward(
        0, token_slots[:2], vectors, weights, docs, table, carried, (cot_near, cot_side)
    )
    _, parts = plane_sum(own_part, near_part, side_part, far_part)
    hidden, normed_two = norm_forward(tokens, parts, vectors)

    two_slots = plane_gather(normed_two)
    both_weights = with_sibling(after(full_both, two_slots[1]))
    cot_far = swap(after(cot_near, two_slots[3]), SECOND)
    raw, mixed, *mixed_there = mlp_forward(two_slots, both_weights)
    cot_far = after(cot_far, raw)
    cot_slots = [cotangent, cot_near, cot_side, cot_far]
    def across(blocks):
        return [swap(block, SIBLING) for block in blocks]

    pairs = [(([mixed], 0), (cot_slots, 0)), ((across(mixed_there), 0), (across(cot_slots), 0))]
    down_grad = token_product(pairs, mlp, width, us=10)
    down_sum = scatter_z(down_grad)
    down_weights = with_sibling(after(full_down, down_grad))
    mlp_weights = list(zip(both_weights, down_weights))
    both_grads, *far_grads, side_part, far_part = mlp_backward(
        2, cot_slots[2:], raw, mlp_weights, (), (down_grad,)
    )
    both_grads, *near_grads, own_part, near_part = mlp_backward(
        0, cot_slots[:2], raw, mlp_weights, (both_grads,)
    )
    near_low, parts = plane_sum(own_part, near_part, side_part, far_part)
    pairs = [
        ((two_slots, 0), ([both_grads], 0)),
        ((across(two_slots), 0), (across([*near_grads, *far_grads]), 0)),
    ]
    both_grad = token_product(pairs, width, 2 * mlp, (near_low,), us=25)
    both_sum = scatter_z(both_grad)
    def whole_rows(half):
        other = swap(half, ACROSS_X)
        odd = x_index == 1
        return jnp.concatenate(
            [jnp.where(odd, other, half), jnp.where(odd, half, other)], 0
        ).astype(jnp.float32)

    grad_hidden, hidden_low, norm_sums = norm_backward(
        hidden, cotangent, parts, vectors, 1, True, (both_grad,)
    )
    near_hidden = swap(hidden_low, FIRST)
    out_parts = mlp_output(mixed, mixed_there, down_weights, (hidden_low,))

    near_hidden = after(near_hidden, out_parts[0])
    side_hidden = swap(after(hidden_low, near_hidden), SECOND)
    far_hidden = swap(near_hidden, SECOND)
    hidden_slots = [hidden_low, near_hidden, side_hidden, far_hidden]
    sums = jnp.zeros((1, 2 * width + 6 * head_cols), jnp.float32)
    common = (weights, docs, table, (proj, lse))
    grad_proj, sums, *near_proj, own_part, near_part = attention_backward(
        0, hidden_slots[:2], token_slots[:2], *common, sums, (), (out_parts[0],)
    )
    done = (own_part, *hidden_slots[2:])
    out_parts = [*out_parts[:2], *(after(part, *done) for part in out_parts[2:])]
    out_near, out_sum = plane_sum(*out_parts)
    grad_proj, sums, *far_proj, side_part, far_part = attention_backward(
        2, hidden_slots[2:], token_slots[2:], *common, sums, (grad_proj,)
    )

    placed = jnp.zeros((3 * groups, 4, 2, unit), jnp.float32)
    for k in range(2):
        piece_sum = sums[0, 2 * width + 3 * head_cols * k :][: 3 * head_cols]
        placed = lax.dynamic_update_slice(
            placed,
            piece_sum.reshape(3 * groups, 1, 1, unit),
            (0, yc_index ^ k, x_index, 0),
        )
    lines = [v[0, i * width : (i + 1) * width] for v in (sums, norm_sums) for i in range(2)]
    lines = [v.reshape(planes, 4, rows) for v in lines] + [placed.reshape(planes, 4, 3 * rows)]
    extra = jnp.concatenate(lines, 2).reshape(planes, 28 * rows)
    extra = jnp.pad(extra, ((0, 0), (0, EXTRA_ROWS * 3 * head_cols - 28 * rows)))
    extra = extra.reshape(planes * EXTRA_ROWS, 3 * head_cols).astype(jnp.bfloat16)
    pairs = [
        (([normed_low], 0), ([grad_proj], 0)),
        ((across([normed_low]), 0), (across([*near_proj, *far_proj]), 0)),
    ]
    qkv_grad = token_product(pairs, width, 3 * head_cols, (out_near,), extra)
    qkv_sum = scatter_z(qkv_grad)
    own, side, near = (part.astype(jnp.float32) for part in out_sum)
    activations = (hidden + (own + side + near)).astype(jnp.bfloat16)
    far_part, side_part = (after(part, qkv_grad) for part in (far_part, side_part))
    norm_near, parts = plane_sum(own_part, near_part, side_part, far_part)
    (d_tokens,) = norm_backward(tokens, grad_hidden, parts, vectors, 0, False)
    def whole_columns(summed):
        half = plane_rows(split_blocks(summed, yc_index, rows))
        other = swap(half, ACROSS_X)
        return [v.reshape(4, rows, summed.shape[1]) for v in (half, other)]

    owned_down = whole_rows(after(down_sum, out_near))
    gate_half, other = whole_columns(both_sum)
    def out_product(window, later):
        pairs = [(([attended_low], window), (hidden_slots, 0))]
        return token_product(pairs, head_cols, width, later, us=40)

    out_there = swap(out_product(1, (gate_half, norm_near, owned_down)), SIBLING)
    out_grad = out_product(0, ()).astype(jnp.float32) + out_there.astype(jnp.float32)
    out_grad = out_grad.astype(jnp.bfloat16)

    if spread:
        owned_out = whole_rows(scatter_z(out_grad))
    else:
        placed_out = lax.dynamic_update_slice(
            jnp.zeros((4, 2, unit, width), jnp.bfloat16),
            out_grad[None, None],
            (yc_index, x_index, 0, 0),
        )
        owned_out = lax.psum_scatter(
            placed_out.reshape(width, width), ("z", "y", "c"), scatter_dimension=0, tiled=True
        )
        owned_out = lax.psum(owned_out, "x").astype(jnp.float32)

    owned_gate, owned_up = spread_columns(gate_half, other, x_index, unpair, planes, piece)
    small = qkv_sum[4 * rows :].reshape(-1)[: 28 * rows].reshape(4, 7 * rows).astype(jnp.float32)
    for axis in ("c", "y", "x"):
        small = small + meet(small, axis, 1, 2)
    small = pick_yc(small, 0)
    half, other = whole_columns(after(qkv_sum, other, parts[2], out_sum[2]))
    (owned_qkv,) = spread_columns(half, other, x_index, lambda v: (v,), 3 * groups, unit)

    return (
        activations,
        d_tokens,
        small[:rows],
        small[rows : 2 * rows],
        owned_qkv,
        small[4 * rows :],
        owned_out,
        small[2 * rows : 3 * rows],
        small[3 * rows : 4 * rows],
        owned_gate,
        owned_up,
        owned_down,
    )


def solution(mesh):
    reps, shards = mesh.shape["rep"], mesh.shape["shard"]
    grid = Mesh(mesh.devices.reshape(reps, shards // 4, 2, 2), EVERY)
    tokens, rows, vector = P(EVERY, None), P(("z", "y", "c"), None), P(("z", "y", "c"))
    return jax.shard_map(
        per_device,
        mesh=grid,
        in_specs=(
            tokens,
            P(EVERY),
            tokens,
            vector,
            vector,
            rows,
            vector,
            rows,
            vector,
            vector,
            rows,
            rows,
            rows,
        ),
        out_specs=(
            tokens,
            tokens,
            vector,
            vector,
            rows,
            vector,
            rows,
            vector,
            vector,
            rows,
            rows,
            rows,
        ),
        check_vma=False,
    )
```

```python
import jax
import jax.numpy as jnp
from jax import lax
from jax.experimental import pallas as pl
from jax.experimental.pallas import tpu as pltpu
from jax.sharding import Mesh, PartitionSpec as P

HEAD_DIM = 64
ROT = 16
PLANE = ("x", "y", "c")
EVERY = ("x", "z", "y", "c")
SIBLING = (1, 1)
FIRST = (4, 2)
SECOND = (2, 4)
ACROSS_X = (4, 4)
ACROSS_Y = (2, 2)
ACROSS_YC = (3, 3)
VMEM_BYTES = 48 << 20
EXTRA_ROWS = 16
MICROSECONDS = {
    "attention_forward": 15,
    "attention_backward": 27,
    "mlp_forward": 8,
    "mlp_backward": 21,
    "mlp_output": 18,
    "token_product": 14,
    "norm_forward": 5,
    "norm_backward": 5,
    "spread_columns": 4,
    "pick_columns": 3,
    "place_blocks": 1,
    "split_blocks": 1,
    "unpack_vectors": 1,
    "after": 0,
}


def cost(name):
    return cost_of(MICROSECONDS[name])


def cost_of(us):
    flops = us * 1_150_000_000 + 1_000_000
    return pl.CostEstimate(flops=flops, bytes_accessed=1 << 10, transcendentals=0)


def swap(values, masks):
    pairs = [(i, i ^ masks[i & 1]) for i in range(8)]
    return lax.ppermute(values, PLANE, pairs)


def plane_gather(values):
    side = swap(values, SECOND)
    near = after(swap(values, FIRST), side)
    return [values, near, side, swap(near, SECOND)]


def plane_sum(own, near, side, far, later=()):
    far = swap(far, SECOND)
    side = swap(side, SECOND)
    near = after((near + far.astype(jnp.float32)).astype(jnp.bfloat16), side, *later)

    return near, (own, side, swap(near, FIRST))


def with_sibling(values):
    return [values, swap(values, SIBLING)]


def exchange(blocks, later=()):
    if later:
        blocks = [blocks[0]] + [after(block, *later) for block in blocks[1:]]
    blocks, masks = list(blocks), (None, SIBLING, ACROSS_Y, ACROSS_YC)
    return blocks[:1] + [swap(blocks[k], masks[k]) for k in range(1, 4)]


def meet(values, axis, bit, size):
    return lax.ppermute(values, axis, [(i, i ^ bit) for i in range(size)])


def gather_direct(block, axis, size):
    parts = [block] + [meet(block, axis, k, size) for k in range(1, size)]
    return place_blocks(parts, lax.axis_index(axis))


def layer_norm(values, gain_vec, bias_vec):
    average = jnp.mean(values, -1, keepdims=True)
    centered = values - average
    recip_std = lax.rsqrt(jnp.mean(centered * centered, -1, keepdims=True) + 1e-05)
    unit_vals = centered * recip_std
    return (unit_vals * gain_vec + bias_vec, unit_vals, recip_std)


def norm_back(grad_in, unit_vals, recip_std, gain_vec):
    scaled = grad_in * gain_vec
    return recip_std * (
        scaled
        - jnp.mean(scaled, -1, keepdims=True)
        - unit_vals * jnp.mean(scaled * unit_vals, -1, keepdims=True)
    )


def dot(left, right):
    return jnp.dot(left, right, preferred_element_type=jnp.float32)


def contract_last(left, right):
    return lax.dot_general(
        left, right, (((1,), (1,)), ((), ())), preferred_element_type=jnp.float32
    )


def contract_first(left, right):
    return lax.dot_general(
        left, right, (((0,), (0,)), ((), ())), preferred_element_type=jnp.float32
    )


def spread_rotary(positions):
    half_rot = ROT // 2
    frequency = 10000.0 ** (-(jnp.arange(half_rot, dtype=jnp.float32) * 2.0 / ROT))
    lane = jnp.arange(2 * HEAD_DIM) % HEAD_DIM
    frequency = jnp.where(lane < ROT, jnp.tile(frequency, 2 * HEAD_DIM // half_rot), 0.0)
    angles = positions.astype(jnp.float32)[:, None] * frequency
    sine = jnp.sin(angles)
    from_right = jnp.where(lane < half_rot, -sine, 0.0)
    from_left = jnp.where(lane < half_rot, 0.0, sine)
    return jnp.concatenate([jnp.cos(angles), from_right, from_left], 1)


def turn(values, table, direction):
    cols, lanes = values.shape[1], 2 * HEAD_DIM
    times = cols // lanes
    wide = [jnp.concatenate([table[:, k * lanes : (k + 1) * lanes]] * times, 1) for k in range(3)]
    half_rot = ROT // 2
    from_right = pltpu.roll(values, cols - half_rot, 1) * wide[1]
    from_left = pltpu.roll(values, half_rot, 1) * wide[2]
    return values * wide[0] + direction * (from_right + from_left)


def head_mask(head, shape):
    lane = lax.broadcasted_iota(jnp.int32, shape, 1)
    return (lane >= head * HEAD_DIM) & (lane < (head + 1) * HEAD_DIM)


def visible(docs_col, docs_row):
    shape = (docs_col.shape[0], docs_row.shape[1])
    row = lax.broadcasted_iota(jnp.int32, shape, 0)
    col = lax.broadcasted_iota(jnp.int32, shape, 1)
    return (docs_col == docs_row) & (col <= row)


def by_head(values):
    heads = values.shape[1] // HEAD_DIM
    zero = jnp.zeros_like(values)
    return jnp.concatenate(
        [jnp.where(head_mask(head, values.shape), values, zero) for head in range(heads)], 0
    )


def join_heads(stacked):
    heads = stacked.shape[1] // HEAD_DIM
    rows = stacked.shape[0] // heads
    joined = stacked[:rows]
    for head in range(1, heads):
        part = stacked[head * rows : (head + 1) * rows]
        joined = jnp.where(head_mask(head, part.shape), part, joined)
    return joined


def head_scores(query_heads, key, allowed):
    return jnp.where(allowed, contract_last(query_heads, key) * 0.125, -1e30)


def pick_slot(step, slots, place):
    for k, slot in enumerate(slots):

        @pl.when(step == k)
        def _(slot=slot):
            place[...] = slot[...]


def put_slot(step, value, slots):
    for k, slot in enumerate(slots):

        @pl.when(step == k)
        def _(slot=slot):
            slot[...] = value.astype(slot.dtype)


def loader(step, sources, places, sems, order=(0,)):
    def fetch(which, k):
        return pltpu.make_async_copy(sources[which][k], places[k].at[which], sems.at[which, k])

    @pl.when(step == 0)
    def _():
        for which in range(2):
            for k in order:
                fetch(which, k).start()

    def wait(which, k=0):
        @pl.when(step == 0)
        def _():
            fetch(which, k).wait()

    return wait


def forward_kernel(first, *refs):
    slots, refs = refs[:2], refs[2:]
    vectors, docs_col, docs_row, table = refs[:4]
    weights = [refs[4:6], refs[6:8]]
    outs, (place, weight, weight_out, sems) = refs[-10:-4], refs[-4:]
    normed, proj, lse, attended = outs[:4]
    step = pl.program_id(0)
    wait = loader(step, weights, [weight, weight_out], sems, (0, 1))
    pick_slot(step, slots, place)
    width = normed.shape[1]
    gain, bias = vectors[:1, :width], vectors[:1, width : 2 * width]
    values, _, _ = layer_norm(place[...].astype(jnp.float32), gain, bias)
    low = values.astype(jnp.bfloat16)
    normed[...] = low
    allowed = visible(docs_col[0], docs_row[0])
    allowed = jnp.concatenate([allowed] * (weight_out.shape[1] // HEAD_DIM), 0)
    lane = lax.broadcasted_iota(jnp.int32, lse.shape, 1)
    logs = jnp.zeros(lse.shape, jnp.float32)
    partial = 0.0
    cols = weight_out.shape[1]
    heads = cols // HEAD_DIM
    for which in range(2):
        wait(which)
        start = 4 * width + 3 * cols * which
        whole = dot(low, weight[which]) + vectors[:1, start : start + 3 * cols]
        turned = turn(whole[:, : 2 * cols], table[...], 1.0)
        turned = turned.astype(jnp.bfloat16)
        query, key = turned[:, :cols], turned[:, cols:]
        value = whole[:, 2 * cols :].astype(jnp.bfloat16)
        start = 3 * cols * which
        proj[:, start : start + 2 * cols] = turned
        proj[:, start + 2 * cols : start + 3 * cols] = value
        scores = head_scores(by_head(query), key, allowed)
        highest = jnp.max(scores, -1, keepdims=True)
        powers = jnp.exp(scores - highest)
        total = jnp.sum(powers, -1, keepdims=True)
        probs = (powers * (1.0 / total)).astype(jnp.bfloat16)
        joined = join_heads(dot(probs, value))
        log_total = highest + jnp.log(total)
        rows = query.shape[0]
        for head in range(heads):
            part = log_total[head * rows : (head + 1) * rows]
            logs = jnp.where(lane == heads * which + head, part, logs)
        low_joined = joined.astype(jnp.bfloat16)
        attended[:, cols * which : cols * (which + 1)] = low_joined
        wait(which, 1)
        partial += dot(low_joined, weight_out[which])
    lse[...] = logs
    put_slot(step, partial, outs[4:])


def backward_kernel(count, *refs):
    slots, tokens, refs = refs[:count], refs[count : 2 * count], refs[2 * count :]
    docs_col, docs_row, table, proj, lse, sums_in = refs[:6]
    weights = [refs[6:8], refs[8:10]]
    outs, (place, inputs, weight, weight_out, sems) = refs[-7 - 2 * count : -5], refs[-5:]
    dproj, sums, dproj_there = outs[0], outs[1], outs[2 : 2 + count]
    step = pl.program_id(0)
    wait = loader(step, weights, [weight, weight_out], sems, (1, 0))
    pick_slot(step, slots, place)
    pick_slot(step, tokens, inputs)

    @pl.when(step == 0)
    def _():
        sums[...] = sums_in[...]

    grad = place[...]
    cols = weight_out.shape[1]
    heads = cols // HEAD_DIM
    allowed = visible(docs_col[0], docs_row[0])
    allowed = jnp.concatenate([allowed] * heads, 0)
    width = grad.shape[1]
    dnorm = 0.0
    for which in range(2):
        wait(which, 1)
        datt = contract_last(grad, weight_out[which]).astype(jnp.bfloat16)
        start = 3 * cols * which
        query, key, value = (
            proj[:, start + i * cols : start + (i + 1) * cols] for i in range(3)
        )
        query_heads, datt_heads = by_head(query), by_head(datt)
        scores = head_scores(query_heads, key, allowed)
        log_total = jnp.concatenate(
            [lse[:, heads * which + head : heads * which + head + 1] for head in range(heads)], 0
        )
        probs = jnp.exp(scores - log_total)
        dvalue = contract_first(probs.astype(jnp.bfloat16), datt_heads)
        dprobs = contract_last(datt_heads, value)
        inner = jnp.sum(probs * dprobs, -1, keepdims=True)
        dscores = (0.125 * probs * (dprobs - inner)).astype(jnp.bfloat16)
        dquery = join_heads(dot(dscores, key))
        dkey = contract_first(dscores, query_heads)
        turned = turn(jnp.concatenate([dquery, dkey], 1), table[...], -1.0)
        low = jnp.concatenate([turned, dvalue], 1).astype(jnp.bfloat16)
        if which == 0:
            dproj[...] = low
        else:
            put_slot(step, low, dproj_there)
        wait(which)
        dnorm += contract_last(low, weight[which])
        start += 2 * width
        sums[:, start : start + 3 * cols] += jnp.sum(low.astype(jnp.float32), 0, keepdims=True)
    put_slot(step, dnorm, outs[2 + count :])
    values = inputs[...].astype(jnp.float32)
    centered = values - jnp.mean(values, -1, keepdims=True)
    unit = centered * lax.rsqrt(jnp.mean(centered * centered, -1, keepdims=True) + 1e-05)
    sums[:, :width] += jnp.sum(dnorm * unit, 0, keepdims=True)
    sums[:, width : 2 * width] += jnp.sum(dnorm, 0, keepdims=True)


def standardized(values):
    centered = values - jnp.mean(values, -1, keepdims=True)
    recip_std = lax.rsqrt(jnp.mean(centered * centered, -1, keepdims=True) + 1e-05)
    return centered * recip_std, recip_std


def norm_forward(tokens, parts, vectors):
    length, width = tokens.shape
    step = length // 4

    def kernel(token_ref, own, side, near, vec, hidden, low):
        total = own[...] + side[...].astype(jnp.float32) + near[...].astype(jnp.float32)
        total += token_ref[...].astype(jnp.float32)
        hidden[...] = total
        unit, _ = standardized(total)
        gain, bias = vec[:1, 2 * width : 3 * width], vec[:1, 3 * width : 4 * width]
        low[...] = (unit * gain + bias).astype(jnp.bfloat16)

    block = moving((step, width), 0)
    return run_kernel(
        kernel,
        "norm_forward",
        4,
        [tokens, *parts, vectors],
        [block] * 4 + [fixed(vectors.shape)],
        [jax.ShapeDtypeStruct((length, width), d) for d in (jnp.float32, jnp.bfloat16)],
        [block] * 2,
        [],
        {},
    )


def norm_backward(values, straight, parts, vectors, which, with_sums, later=()):
    length, width = values.shape
    step = length // 4

    def kernel(value_ref, straight_ref, own, side, near, vec, total, *more):
        grad = own[...] + side[...].astype(jnp.float32) + near[...].astype(jnp.float32)
        unit, recip_std = standardized(value_ref[...].astype(jnp.float32))
        gain = vec[:1, 2 * which * width : (2 * which + 1) * width]
        back = norm_back(grad, unit, recip_std, gain)
        back += straight_ref[...].astype(jnp.float32)
        total[...] = back
        if with_sums:
            low, sums = more
            low[...] = back.astype(jnp.bfloat16)

            @pl.when(pl.program_id(0) == 0)
            def _():
                sums[...] = jnp.zeros_like(sums)

            sums[:, :width] += jnp.sum(grad * unit, 0, keepdims=True)
            sums[:, width:] += jnp.sum(grad, 0, keepdims=True)

    block = moving((step, width), 0)
    shape = jax.ShapeDtypeStruct
    shapes, specs = [shape((length, width), jnp.float32)], [block]
    if with_sums:
        shapes += [shape((length, width), jnp.bfloat16), shape((1, 2 * width), jnp.float32)]
        specs += [block, fixed((1, 2 * width))]
    return run_kernel(
        kernel,
        "norm_backward",
        4,
        [values, straight, *parts, vectors],
        [block] * 5 + [fixed(vectors.shape)],
        shapes,
        specs,
        [],
        {},
        later,
    )


def fixed(shape):
    return pl.BlockSpec(shape, lambda i: (0,) * len(shape))


def moving(shape, first):
    return pl.BlockSpec(shape, lambda i: (first + i,) + (0,) * (len(shape) - 1))


def anywhere(count):
    return [pl.BlockSpec(memory_space=pl.ANY)] * count


def run_kernel(
    kernel, name, blocks, inputs, in_specs, shapes, out_specs, scratch, aliases, later=(), us=None
):
    given, used = len(later), kernel
    if given:

        def used(*refs):
            kernel(*refs[given:])

    aliases = {k + given: v for k, v in aliases.items()}
    return pl.pallas_call(
        used,
        grid=(blocks,),
        out_shape=shapes,
        in_specs=anywhere(given) + in_specs,
        out_specs=out_specs,
        scratch_shapes=scratch,
        input_output_aliases=aliases,
        compiler_params=pltpu.CompilerParams(vmem_limit_bytes=VMEM_BYTES),
        cost_estimate=cost(name) if us is None else cost_of(us),
        name=name,
    )(*later, *inputs)


def after(value, *others, us=0):
    return pl.pallas_call(
        lambda *refs: None,
        out_shape=jax.ShapeDtypeStruct(value.shape, value.dtype),
        in_specs=anywhere(1 + len(others)),
        out_specs=pl.BlockSpec(memory_space=pl.ANY),
        input_output_aliases={0: 0},
        cost_estimate=cost_of(us),
        name="after",
    )(value, *others)


def part_types(first):
    return jnp.bfloat16 if first >= 2 else jnp.float32


def attention_forward(first, slots, vectors, weights, docs, table, carried, later=()):
    length, width = slots[0].shape
    cols = weights[0][1].shape[0]
    shape = jax.ShapeDtypeStruct
    shapes = [
        shape((4 * length, width), jnp.bfloat16),
        shape((4 * length, 6 * cols), jnp.bfloat16),
        shape((4 * length, 128), jnp.float32),
        shape((4 * length, 2 * cols), jnp.bfloat16),
    ] + [shape((length, width), part_types(first))] * 2
    inputs = [*slots, vectors, *docs, table, *weights[0], *weights[1], *carried]
    in_specs = (
        [fixed((length, width))] * 2
        + [fixed(vectors.shape)]
        + [moving((1, length, 1), first), moving((1, 1, length), first)]
        + [moving((length, table.shape[1]), first)]
        + anywhere(4 + len(carried))
    )
    out_specs = [moving((length, s.shape[1]), first) for s in shapes[:4]]
    out_specs += [fixed((length, width))] * 2
    scratch = [
        pltpu.VMEM((length, width), jnp.bfloat16),
        pltpu.VMEM((2,) + weights[0][0].shape, jnp.bfloat16),
        pltpu.VMEM((2,) + weights[0][1].shape, jnp.bfloat16),
        pltpu.SemaphoreType.DMA((2, 2)),
    ]
    aliases = {len(inputs) - len(carried) + i: i for i in range(len(carried))}

    def kernel(*refs):
        forward_kernel(first, *refs)

    return run_kernel(
        kernel,
        "attention_forward",
        2,
        inputs,
        in_specs,
        shapes,
        out_specs,
        scratch,
        aliases,
        later,
    )


def attention_backward(
    first, slots, tokens, weights, docs, table, kept, sums, carried, later=()
):
    length, width = slots[0].shape
    cols, count = weights[0][1].shape[0], len(slots)
    shape = jax.ShapeDtypeStruct
    shapes = [shape((4 * length, 3 * cols), jnp.bfloat16), shape(sums.shape, jnp.float32)]
    shapes += [shape((length, 3 * cols), jnp.bfloat16)] * count
    shapes += [shape((length, width), part_types(first))] * count
    inputs = [*slots, *tokens, *docs, table, *kept, sums, *weights[0], *weights[1], *carried]
    in_specs = (
        [fixed((length, width))] * (2 * count)
        + [moving((1, length, 1), first), moving((1, 1, length), first)]
        + [moving((length, table.shape[1]), first)]
        + [moving((length, k.shape[1]), first) for k in kept]
        + [fixed(sums.shape)]
        + anywhere(4 + len(carried))
    )
    out_specs = [moving((length, 3 * cols), first)] + [fixed(s.shape) for s in shapes[1:]]
    scratch = [pltpu.VMEM((length, width), jnp.bfloat16)] * 2 + [
        pltpu.VMEM((2,) + weights[0][0].shape, jnp.bfloat16),
        pltpu.VMEM((2,) + weights[0][1].shape, jnp.bfloat16),
        pltpu.SemaphoreType.DMA((2, 2)),
    ]

    def kernel(*refs):
        backward_kernel(count, *refs)

    return run_kernel(
        kernel,
        "attention_backward",
        count,
        inputs,
        in_specs,
        shapes,
        out_specs,
        scratch,
        {len(inputs) - len(carried): 0} if carried else {},
        later,
    )


def token_product(pairs, rows, cols, later=(), extra=None, us=None):
    by_rows, step = rows % 512 == 0, 512
    if extra is not None:
        step = rows * EXTRA_ROWS // extra.shape[0]
    grid = (rows if by_rows else cols) // step

    def fixed_columns(length, size, window):
        return pl.BlockSpec((length, size), lambda i: (0, window))

    def step_columns(length, window):
        return pl.BlockSpec((length, step), lambda i: (0, window * grid + i))

    sides, inputs, specs = [[], []], [], []
    for pair in pairs:
        for side, (blocks, window) in enumerate(pair):
            for block in blocks:
                sides[side].append((len(inputs), block.shape[0]))
                inputs.append(block)
                if by_rows == (side == 0):
                    specs.append(step_columns(block.shape[0], window))
                else:
                    specs.append(fixed_columns(block.shape[0], (rows, cols)[side], window))
    tokens = sum(length for _, length in sides[0])
    shape, place = (rows, cols), pl.BlockSpec((step, cols), lambda i: (i, 0))
    if not by_rows:
        place = pl.BlockSpec((rows, step), lambda i: (0, i))
    if extra is not None:
        inputs, specs = inputs + [extra], specs + [moving((EXTRA_ROWS, cols), 0)]
        place = moving((step + EXTRA_ROWS, cols), 0)
        shape = (rows + extra.shape[0], cols)

    def kernel(*refs):
        out, left, right = refs[-3:]

        def fill(side, whole):
            start = 0
            for k, length in sides[side]:
                whole[start : start + length, :] = refs[k][...]
                start += length

        moved, kept = (0, 1) if by_rows else (1, 0)
        wholes = (left, right)
        fill(moved, wholes[moved])

        @pl.when(pl.program_id(0) == 0)
        def _():
            fill(kept, wholes[kept])

        total = contract_first(left[...], right[...]).astype(out.dtype)
        if extra is None:
            out[...] = total
        else:
            out[:step, :] = total
            out[step:, :] = refs[-4][...]

    left_cols, right_cols = (step, cols) if by_rows else (rows, step)
    return run_kernel(
        kernel,
        "token_product",
        grid,
        inputs,
        specs,
        jax.ShapeDtypeStruct(shape, jnp.bfloat16),
        place,
        [pltpu.VMEM((tokens, size), jnp.bfloat16) for size in (left_cols, right_cols)],
        {},
        later,
        us,
    )


def spread_columns(half, other, x_index, split, outer, size):
    blocks, rows, cols = half.shape
    width = 8 * outer * size
    outs = len(split(jnp.zeros((8, cols), jnp.float32)))
    step = min(rows, 32)

    def kernel(x_ref, half_ref, other_ref, *out_refs):
        here = x_ref[0]
        for t in range(blocks):
            mine, theirs = half_ref[t].astype(jnp.float32), other_ref[t].astype(jnp.float32)
            for x in range(2):
                columns = split(jnp.where(here == x, mine, theirs))
                for out, values in zip(out_refs, columns):
                    for k in range(outer):
                        start = ((k * blocks + t) * 2 + x) * size
                        out[:, start : start + size] = values[:, k * size : (k + 1) * size]

    block = pl.BlockSpec((blocks, step, cols), lambda i: (0, i, 0))
    return run_kernel(
        kernel,
        "spread_columns",
        rows // step,
        [scalar(x_index), half, other],
        [pl.BlockSpec(memory_space=pltpu.SMEM), block, block],
        [jax.ShapeDtypeStruct((rows, width), jnp.float32)] * outs,
        [pl.BlockSpec((step, width), lambda i: (i, 0))] * outs,
        [],
        {},
    )


def last_tile(values, start):
    tile = values[:, start:]
    return tile, pltpu.roll(tile, HEAD_DIM, 1)


def hidden_kernel(*refs):
    slots, weights, refs = refs[:4], refs[4:6], refs[6:]
    raw, mixed, mixed_there, (place, weight, sems) = refs[0], refs[1], refs[2:6], refs[6:]
    step = pl.program_id(0)
    wait = loader(step, [weights[:1], weights[1:]], [weight], sems)
    pick_slot(step, slots, place)
    cols, hidden = weight.shape[2], mixed.shape[1]
    main = hidden // 128 * 128

    def mix(gate, up):
        return (gate * jax.nn.sigmoid(gate) * up).astype(jnp.bfloat16)

    for which in range(2):
        wait(which)
        both = dot(place[...], weight[which])
        raw[:, which * cols : (which + 1) * cols] = both
        pieces = [mix(both[:, :main], both[:, main : 2 * main])]
        if main < hidden:
            pieces.append(mix(*last_tile(both, 2 * main))[:, : hidden - main])
        low = jnp.concatenate(pieces, 1)
        if which == 0:
            mixed[...] = low
        else:
            put_slot(step, low, mixed_there)


def hidden_back_kernel(*refs):
    slots, raw, refs = refs[:2], refs[2], refs[3:]
    weights = [refs[0:2], refs[2:4]]
    grads, grads_there, outs = refs[-9], refs[-8:-6], refs[-6:-4]
    grad_out, weight, weight_down, sems = refs[-4:]
    step = pl.program_id(0)
    wait = loader(step, weights, [weight, weight_down], sems, (1, 0))
    pick_slot(step, slots, grad_out)
    cols, hidden = weight.shape[2], weight_down.shape[1]
    main = hidden // 128 * 128

    def gradients(gate, up, dm):
        sig = jax.nn.sigmoid(gate)
        return dm * up * sig * (1.0 + gate * (1.0 - sig)), dm * gate * sig

    partial = 0.0
    for which in range(2):
        wait(which, 1)
        dmixed = contract_last(grad_out[...], weight_down[which])
        both = raw[:, which * cols : (which + 1) * cols]
        pieces = list(gradients(both[:, :main], both[:, main : 2 * main], dmixed[:, :main]))
        if main < hidden:
            gate, up = last_tile(both, 2 * main)
            rest = dmixed[:, main:]
            dgate, dup = gradients(gate, up, jnp.concatenate([rest, rest], 1))
            lane = lax.broadcasted_iota(jnp.int32, dgate.shape, 1)
            pieces.append(jnp.where(lane < HEAD_DIM, dgate, pltpu.roll(dup, HEAD_DIM, 1)))
        low = jnp.concatenate(pieces, 1).astype(jnp.bfloat16)
        if which == 0:
            grads[...] = low
        else:
            put_slot(step, low, grads_there)
        wait(which)
        partial += contract_last(low, weight[which])
    put_slot(step, partial, outs)


def mlp_forward(slots, weights):
    length, width = slots[0].shape
    both = weights[0].shape[1]
    shape = jax.ShapeDtypeStruct
    shapes = [
        shape((4 * length, 2 * both), jnp.float32),
        shape((4 * length, both // 2), jnp.bfloat16),
    ] + [shape((length, both // 2), jnp.bfloat16)] * 4
    scratch = [
        pltpu.VMEM((length, width), jnp.bfloat16),
        pltpu.VMEM((2,) + weights[0].shape, jnp.bfloat16),
        pltpu.SemaphoreType.DMA((2, 1)),
    ]
    return run_kernel(
        hidden_kernel,
        "mlp_forward",
        4,
        [*slots, *weights],
        [fixed((length, width))] * 4 + anywhere(2),
        shapes,
        [moving((length, s.shape[1]), 0) for s in shapes[:2]] + [fixed(s.shape) for s in shapes[2:]],
        scratch,
        {},
    )


def mlp_backward(first, slots, raw, weights, carried, later=()):
    length, width = slots[0].shape
    both = weights[0][0].shape[1]
    shape = jax.ShapeDtypeStruct
    shapes = [shape((4 * length, both), jnp.bfloat16)]
    shapes += [shape((length, both), jnp.bfloat16)] * 2
    shapes += [shape((length, width), part_types(first))] * 2
    inputs = [*slots, raw, *weights[0], *weights[1], *carried]
    scratch = [
        pltpu.VMEM((length, width), jnp.bfloat16),
        pltpu.VMEM((2,) + weights[0][0].shape, jnp.bfloat16),
        pltpu.VMEM((2,) + weights[0][1].shape, jnp.bfloat16),
        pltpu.SemaphoreType.DMA((2, 2)),
    ]

    def kernel(*refs):
        hidden_back_kernel(*refs[:7], *refs[7 + len(carried) :])

    return run_kernel(
        kernel,
        "mlp_backward",
        2,
        inputs,
        [fixed((length, width))] * 2
        + [moving((length, 2 * both), first)]
        + anywhere(4 + len(carried)),
        shapes,
        [moving((length, both), first)] + [fixed(s.shape) for s in shapes[1:]],
        scratch,
        {7 + i: i for i in range(len(carried))},
        later,
    )


def mlp_output(mixed, mixed_there, weights, later=()):
    hidden, width = weights[0].shape
    length = mixed.shape[0] // 4

    def kernel(*refs):
        slots, outs, (place, weight, sems) = refs[1:5], refs[7:11], refs[11:]
        step = pl.program_id(0)
        wait = loader(step, [refs[5:6], refs[6:7]], [weight], sems)
        pick_slot(step, slots, place)
        partial = 0.0
        for which, values in enumerate((refs[0], place)):
            wait(which)
            partial += dot(values[...], weight[which])
        put_slot(step, partial, outs)

    return run_kernel(
        kernel,
        "mlp_output",
        4,
        [mixed, *mixed_there, *weights],
        [moving((length, hidden), 0)] + [fixed((length, hidden))] * 4 + anywhere(2),
        [jax.ShapeDtypeStruct((length, width), part_types(k)) for k in range(4)],
        [fixed((length, width))] * 4,
        [
            pltpu.VMEM((length, hidden), jnp.bfloat16),
            pltpu.VMEM((2, hidden, width), jnp.bfloat16),
            pltpu.SemaphoreType.DMA((2, 1)),
        ],
        {},
        later,
    )


def scalar(value):
    return value.reshape(1).astype(jnp.int32)


def place_blocks(parts, index):
    length, width = parts[0].shape

    def kernel(index_ref, *refs):
        for k, part in enumerate(refs[:-1]):
            start = pl.multiple_of((index_ref[0] ^ k) * length, length)
            refs[-1][pl.ds(start, length), :] = part[...]

    return run_kernel(
        kernel,
        "place_blocks",
        1,
        [scalar(index), *parts],
        [pl.BlockSpec(memory_space=pltpu.SMEM)] + [fixed((length, width))] * len(parts),
        jax.ShapeDtypeStruct((len(parts) * length, width), parts[0].dtype),
        fixed((len(parts) * length, width)),
        [],
        {},
    )


def split_blocks(values, index, length):
    width = values.shape[1]

    def kernel(index_ref, ref, *outs):
        for k, out in enumerate(outs):
            start = pl.multiple_of((index_ref[0] ^ k) * length, length)
            out[...] = ref[pl.ds(start, length), :]

    return run_kernel(
        kernel,
        "split_blocks",
        1,
        [scalar(index), values],
        [pl.BlockSpec(memory_space=pltpu.SMEM), fixed(values.shape)],
        [jax.ShapeDtypeStruct((length, width), values.dtype)] * 4,
        [fixed((length, width))] * 4,
        [],
        {},
    )


def pick_columns(weights, x_index, yc_index, outer, size, merge):
    rows, width = weights[0].shape
    cols = merge(*([jnp.zeros((8, outer * size), jnp.float32)] * len(weights))).shape[1]
    step, kind = min(rows, 32), weights[0].dtype

    def kernel(x_ref, yc_ref, *refs):
        sources, outs, stage = refs[: len(weights)], refs[len(weights) : -1], refs[-1]
        here = x_ref[0]
        for t in range(4):
            picked = []
            for source in sources:
                pieces = []
                for k in range(outer):
                    start = (k * 4 + t) * 2 * size
                    both = source[:, start : start + 2 * size].astype(jnp.float32)
                    pieces.append(jnp.where(here == 0, both[:, :size], both[:, size:]))
                picked.append(jnp.concatenate(pieces, 1))
            stage[t ^ yc_ref[0]] = merge(*picked).astype(kind)
        for k, out in enumerate(outs):
            out[...] = stage[k]

    return run_kernel(
        kernel,
        "pick_columns",
        rows // step,
        [scalar(x_index), scalar(yc_index), *weights],
        [pl.BlockSpec(memory_space=pltpu.SMEM)] * 2 + [moving((step, width), 0)] * len(weights),
        [jax.ShapeDtypeStruct((rows, cols), kind)] * 4,
        [moving((step, cols), 0)] * 4,
        [pltpu.VMEM((4, step, cols), kind)],
        {},
    )


def unpack_vectors(packed, shards, x_index, yc_index, outer, size):
    rows = packed.shape[1]
    width, cols = rows * shards, outer * size

    def kernel(x_ref, yc_ref, ref, out, whole, stage):
        for shard in range(shards):
            for k in range(7):
                line = jnp.broadcast_to(ref[shard * 8 + k : shard * 8 + k + 1, :], (8, rows))
                if k < 4:
                    start = k * width + shard * rows
                    out[:, start : start + rows] = line
                else:
                    start = (3 * shard + k - 4) * rows
                    whole[:, start : start + rows] = line
        for t in range(4):
            pieces = []
            for k in range(outer):
                start = (k * 4 + t) * 2 * size
                both = whole[:, start : start + 2 * size]
                pieces.append(jnp.where(x_ref[0] == 0, both[:, :size], both[:, size:]))
            stage[t ^ yc_ref[0]] = jnp.concatenate(pieces, 1)
        for k in range(2):
            start = 4 * width + k * cols
            out[:, start : start + cols] = stage[k]

    shape = (8, 4 * width + 2 * cols)
    return run_kernel(
        kernel,
        "unpack_vectors",
        1,
        [scalar(x_index), scalar(yc_index), packed],
        [pl.BlockSpec(memory_space=pltpu.SMEM)] * 2 + [fixed(packed.shape)],
        jax.ShapeDtypeStruct(shape, jnp.float32),
        fixed(shape),
        [pltpu.VMEM((8, 3 * width), jnp.float32), pltpu.VMEM((4, 8, cols), jnp.float32)],
        {},
    )


def gather_z(values):
    return lax.all_gather(values, "z", axis=0, tiled=True)


def scatter_z(values):
    return lax.psum_scatter(values, "z", scatter_dimension=0, tiled=True)


def per_device(
    tokens,
    doc_ids,
    cotangent,
    ln1_gain,
    ln1_bias,
    w_qkv,
    b_qkv,
    w_out,
    ln2_gain,
    ln2_bias,
    w_gate,
    w_up,
    w_down,
):
    x_index, z_index = lax.axis_index("x"), lax.axis_index("z")
    y_index, c_index = lax.axis_index("y"), lax.axis_index("c")
    yc_index = 2 * y_index + c_index
    planes = lax.axis_size("z")
    shards = 4 * planes
    rows = w_qkv.shape[0]
    width = rows * shards
    hidden_dim = w_gate.shape[1]
    piece = hidden_dim // (2 * shards)
    mlp = piece * planes
    head_cols = width // 8
    spread = rows % (2 * HEAD_DIM) == 0
    groups = planes if spread else 1
    unit = head_cols // groups
    length = tokens.shape[0]

    def pick_x(values, axis):
        return lax.dynamic_index_in_dim(values, x_index, axis, keepdims=False)

    def pick_yc(values, axis):
        return lax.dynamic_index_in_dim(values, yc_index, axis, keepdims=False)

    def plane_rows(blocks, later=()):
        return place_blocks(exchange(blocks, later), yc_index)

    main = mlp // 128 * 128

    def pair(gate, up):
        return jnp.concatenate([gate[:, :main], up[:, :main], gate[:, main:], up[:, main:]], 1)

    def unpair(both):
        rest = both[..., 2 * main :]
        return (
            jnp.concatenate([both[..., :main], rest[..., : mlp - main]], -1),
            jnp.concatenate([both[..., main : 2 * main], rest[..., mlp - main :]], -1),
        )

    blocks = pick_columns([w_qkv], x_index, yc_index, 3 * groups, unit, lambda v: v)
    block_qkv = plane_rows(blocks)
    lines = [v[None] for v in (ln1_gain, ln1_bias, ln2_gain, ln2_bias)]
    lines += [b_qkv.reshape(3, rows), jnp.zeros((1, rows), jnp.bfloat16)]
    packed = after(jnp.concatenate(lines, 0).astype(jnp.float32), blocks[1])
    packed = gather_direct(gather_direct(packed, ("y", "c"), 4), "z", planes)
    if spread:
        full_out = gather_z(pick_x(w_out.reshape(2, rows // 2, width), 0))
    else:
        full_out = lax.all_gather(w_out, ("z", "y", "c"), axis=0, tiled=True)
        full_out = pick_x(pick_yc(full_out.reshape(4, 2, unit, width), 0), 0)
    docs = jnp.stack(plane_gather(doc_ids))
    full_qkv = gather_z(after(block_qkv, full_out))
    token_slots = plane_gather(after(tokens, block_qkv))
    blocks = pick_columns([w_gate, w_up], x_index, yc_index, planes, piece, pair)
    block_both = plane_rows(blocks, (*token_slots[1:3], packed, docs))
    full_both = gather_z(block_both)
    full_down = gather_z(pick_x(w_down.reshape(2, piece, width), 0))

    vectors = unpack_vectors(packed, shards, x_index, yc_index, 3 * groups, unit)
    indices = jnp.arange(length, dtype=jnp.int32)
    same_doc = docs[:, :, None] == docs[:, None, :]
    first_row = jnp.min(jnp.where(same_doc, indices[None, None, :], length), axis=2)
    table = spread_rotary((indices[None] - first_row).reshape(-1))
    docs = (docs[:, :, None], docs[:, None, :])

    full_qkv = after(full_qkv, full_out, block_both, *token_slots[1:], table, *docs, vectors)
    weights = list(zip(with_sibling(full_qkv), with_sibling(full_out)))
    cot_late = after(cotangent, block_both)
    cot_near, cot_side = swap(cot_late, FIRST), swap(cot_late, SECOND)
    *carried, side_part, far_part = attention_forward(
        2, token_slots[2:], vectors, weights, docs, table, ()
    )
    normed_low, proj, lse, attended_low, own_part, near_part = attention_forward(
        0, token_slots[:2], vectors, weights, docs, table, carried, (cot_near, cot_side)
    )
    _, parts = plane_sum(own_part, near_part, side_part, far_part)
    hidden, normed_two = norm_forward(tokens, parts, vectors)

    two_slots = plane_gather(normed_two)
    both_weights = with_sibling(after(full_both, two_slots[1]))
    cot_far = swap(after(cot_near, two_slots[3]), SECOND)
    raw, mixed, *mixed_there = mlp_forward(two_slots, both_weights)
    cot_far = after(cot_far, raw)
    cot_slots = [cotangent, cot_near, cot_side, cot_far]
    def across(blocks):
        return [swap(block, SIBLING) for block in blocks]

    pairs = [(([mixed], 0), (cot_slots, 0)), ((across(mixed_there), 0), (across(cot_slots), 0))]
    down_grad = token_product(pairs, mlp, width, us=10)
    down_sum = scatter_z(down_grad)
    down_weights = with_sibling(after(full_down, down_grad))
    mlp_weights = list(zip(both_weights, down_weights))
    both_grads, *far_grads, side_part, far_part = mlp_backward(
        2, cot_slots[2:], raw, mlp_weights, (), (down_grad,)
    )
    both_grads, *near_grads, own_part, near_part = mlp_backward(
        0, cot_slots[:2], raw, mlp_weights, (both_grads,)
    )
    near_low, parts = plane_sum(own_part, near_part, side_part, far_part)
    pairs = [
        ((two_slots, 0), ([both_grads], 0)),
        ((across(two_slots), 0), (across([*near_grads, *far_grads]), 0)),
    ]
    both_grad = token_product(pairs, width, 2 * mlp, (near_low,), us=25)
    both_sum = scatter_z(both_grad)
    def whole_rows(half):
        other = swap(half, ACROSS_X)
        odd = x_index == 1
        return jnp.concatenate(
            [jnp.where(odd, other, half), jnp.where(odd, half, other)], 0
        ).astype(jnp.float32)

    grad_hidden, hidden_low, norm_sums = norm_backward(
        hidden, cotangent, parts, vectors, 1, True, (both_grad,)
    )
    near_hidden = swap(hidden_low, FIRST)
    out_parts = mlp_output(mixed, mixed_there, down_weights, (hidden_low,))

    near_hidden = after(near_hidden, out_parts[0])
    side_hidden = swap(after(hidden_low, near_hidden), SECOND)
    far_hidden = swap(near_hidden, SECOND)
    hidden_slots = [hidden_low, near_hidden, side_hidden, far_hidden]
    sums = jnp.zeros((1, 2 * width + 6 * head_cols), jnp.float32)
    common = (weights, docs, table, (proj, lse))
    grad_proj, sums, *near_proj, own_part, near_part = attention_backward(
        0, hidden_slots[:2], token_slots[:2], *common, sums, (), (out_parts[0],)
    )
    done = (own_part, *hidden_slots[2:])
    out_parts = [*out_parts[:2], *(after(part, *done) for part in out_parts[2:])]
    out_near, out_sum = plane_sum(*out_parts)
    grad_proj, sums, *far_proj, side_part, far_part = attention_backward(
        2, hidden_slots[2:], token_slots[2:], *common, sums, (grad_proj,)
    )

    placed = jnp.zeros((3 * groups, 4, 2, unit), jnp.float32)
    for k in range(2):
        piece_sum = sums[0, 2 * width + 3 * head_cols * k :][: 3 * head_cols]
        placed = lax.dynamic_update_slice(
            placed,
            piece_sum.reshape(3 * groups, 1, 1, unit),
            (0, yc_index ^ k, x_index, 0),
        )
    lines = [v[0, i * width : (i + 1) * width] for v in (sums, norm_sums) for i in range(2)]
    lines = [v.reshape(planes, 4, rows) for v in lines] + [placed.reshape(planes, 4, 3 * rows)]
    extra = jnp.concatenate(lines, 2).reshape(planes, 28 * rows)
    extra = jnp.pad(extra, ((0, 0), (0, EXTRA_ROWS * 3 * head_cols - 28 * rows)))
    extra = extra.reshape(planes * EXTRA_ROWS, 3 * head_cols).astype(jnp.bfloat16)
    pairs = [
        (([normed_low], 0), ([grad_proj], 0)),
        ((across([normed_low]), 0), (across([*near_proj, *far_proj]), 0)),
    ]
    qkv_grad = token_product(pairs, width, 3 * head_cols, (out_near,), extra)
    qkv_sum = scatter_z(qkv_grad)
    own, side, near = (part.astype(jnp.float32) for part in out_sum)
    activations = (hidden + (own + side + near)).astype(jnp.bfloat16)
    far_part, side_part = (after(part, qkv_grad) for part in (far_part, side_part))
    norm_near, parts = plane_sum(own_part, near_part, side_part, far_part)
    (d_tokens,) = norm_backward(tokens, grad_hidden, parts, vectors, 0, False)
    def whole_columns(summed):
        half = plane_rows(split_blocks(summed, yc_index, rows))
        other = swap(half, ACROSS_X)
        return [v.reshape(4, rows, summed.shape[1]) for v in (half, other)]

    owned_down = whole_rows(after(down_sum, out_near))
    gate_half, other = whole_columns(both_sum)
    out_grad = token_product(
        [(([attended_low], 0), (hidden_slots, 0))],
        2 * head_cols,
        width,
        (gate_half, norm_near, owned_down),
        us=80,
    )
    out_there = swap(out_grad[head_cols:], SIBLING)
    out_grad = out_grad[:head_cols].astype(jnp.float32) + out_there.astype(jnp.float32)
    out_grad = out_grad.astype(jnp.bfloat16)

    if spread:
        owned_out = whole_rows(scatter_z(out_grad))
    else:
        placed_out = lax.dynamic_update_slice(
            jnp.zeros((4, 2, unit, width), jnp.bfloat16),
            out_grad[None, None],
            (yc_index, x_index, 0, 0),
        )
        owned_out = lax.psum_scatter(
            placed_out.reshape(width, width), ("z", "y", "c"), scatter_dimension=0, tiled=True
        )
        owned_out = lax.psum(owned_out, "x").astype(jnp.float32)

    owned_gate, owned_up = spread_columns(gate_half, other, x_index, unpair, planes, piece)
    small = qkv_sum[4 * rows :].reshape(-1)[: 28 * rows].reshape(4, 7 * rows).astype(jnp.float32)
    for axis in ("c", "y", "x"):
        small = small + meet(small, axis, 1, 2)
    small = pick_yc(small, 0)
    half, other = whole_columns(after(qkv_sum, other, parts[2], out_sum[2]))
    (owned_qkv,) = spread_columns(half, other, x_index, lambda v: (v,), 3 * groups, unit)

    return (
        activations,
        d_tokens,
        small[:rows],
        small[rows : 2 * rows],
        owned_qkv,
        small[4 * rows :],
        owned_out,
        small[2 * rows : 3 * rows],
        small[3 * rows : 4 * rows],
        owned_gate,
        owned_up,
        owned_down,
    )


def solution(mesh):
    reps, shards = mesh.shape["rep"], mesh.shape["shard"]
    grid = Mesh(mesh.devices.reshape(reps, shards // 4, 2, 2), EVERY)
    tokens, rows, vector = P(EVERY, None), P(("z", "y", "c"), None), P(("z", "y", "c"))
    return jax.shard_map(
        per_device,
        mesh=grid,
        in_specs=(
            tokens,
            P(EVERY),
            tokens,
            vector,
            vector,
            rows,
            vector,
            rows,
            vector,
            vector,
            rows,
            rows,
            rows,
        ),
        out_specs=(
            tokens,
            tokens,
            vector,
            vector,
            rows,
            vector,
            rows,
            vector,
            vector,
            rows,
            rows,
            rows,
        ),
        check_vma=False,
    )
```
